32 devices in a mesh: days: 2 (over x), sta: 16 (over z, y, core).
Axes of the slice: x: 2, y: 2, z: 4, core: 2. Of those that a mesh axis runs over, the one named last changes fastest.
Arguments:
- records: bfloat16 [384, 256, 256], P(('days', 'sta')), parts along dimension 0, may hold values from -330 to 330
- counts: int32 [128, 4], P(('days', 'sta')), parts along dimension 0, may hold values from 0 to 64
- gap_mask: int32 [128, 256], P(('days', 'sta')), parts along dimension 0, may hold values 0 or 1
Outputs:
- cross_spectra: bfloat16 [7, 2, 384, 12, 128], P(None, None, ('days', 'sta')), parts along dimension 2
The draws below stay inside these ranges and needn't reach their ends.
There are 2 independent parts, one for each index of `days`. The reference program is written for one: setup_inputs(seed, part) draws one part's arguments, and reference() takes and returns one part's arrays. A program takes and returns all parts, laid end to end along the dimension named above; each array names one. Nothing has to cross between parts.
All inputs are finite; a program needn't handle non-finite values. No bound on the sum of `gap_mask` on one device may be relied on, other than what follows from the above.
Results may differ from the reference program's by a relative error of at most 0.0062.
Values may be sent and summed in bfloat16 or wider, within the bound.
A program may use at most 64 MiB of HBM per device.

```python
import math
import jax
import jax.numpy as jnp
from jax import lax

F = 128
SEG_LEN = 256
ST_DEV = 4
CH_DEV = 12
STATIONS = 64
CHANS = 192
HOURS = 4
SEG_H = 64
SEGS = 256
ROUNDS = 3
N_STA = 16


def draw_records(key, part):
    key_noise, key_tilt, key_scale = jax.random.split(key, 3)
    noise = jnp.clip(jax.random.normal(key_noise, (CHANS, SEGS, SEG_LEN), jnp.float32), -6.0, 6.0)
    tilt = jax.random.uniform(key_tilt, (CHANS, 1, 1), jnp.float32, -0.9, 0.9)
    earlier = jnp.concatenate([noise[:, :, -1:], noise[:, :, :-1]], axis=2)
    colored = noise + tilt * earlier
    station_scale = jnp.exp(jax.random.uniform(key_scale, (STATIONS, SEGS, 1), jnp.float32, 0.0, math.log(10.0)))
    station_scale = jnp.repeat(station_scale, 3, axis=0)
    return (colored * station_scale).astype(jnp.bfloat16)


def plant(drawn, rng, smallest, largest):
    extent = drawn.shape
    spot = [jax.random.randint(jax.random.fold_in(rng, axis), (), 0, extent[axis]) for axis in range(len(extent))]
    drawn = drawn.at[tuple(spot)].set(smallest)
    longest = extent.index(max(extent))
    spot[longest] = (spot[longest] + 1) % extent[longest]
    return drawn.at[tuple(spot)].set(largest)


def setup_inputs(seed: int = 0, part: int = 0) -> dict:
    key_of = jax.random.split(jax.random.key(seed), 4)
    part_splits = jax.random.split(jax.random.fold_in(key_of[3], part), 4)
    return {
        "records": draw_records(jax.random.fold_in(jax.random.fold_in(key_of[3], part), 71), part),
        "counts": plant(jax.random.randint(part_splits[1], (STATIONS, HOURS), 0, SEG_H + 1), jax.random.fold_in(part_splits[1], 1), 0, SEG_H).astype(jnp.int32),
        "gap_mask": plant((jax.random.randint(part_splits[2], (STATIONS, SEGS), 0, 8) < 7).astype(jnp.int32), jax.random.fold_in(part_splits[2], 1), 0, 1),
    }


epsilon = 1e-06

def fourier_matrix(samples):
    freq_bins = samples // 2
    times_axis = jnp.arange(samples, dtype=jnp.int32)
    bins_axis = jnp.arange(freq_bins, dtype=jnp.int32)
    phase_idx = times_axis[:, None] * bins_axis[None, :] % samples
    angle = 2.0 * math.pi / samples * phase_idx.astype(jnp.float32)
    taper = 0.5 - 0.5 * jnp.cos(2.0 * math.pi / samples * (times_axis.astype(jnp.float32) + 0.5))
    table_full = jnp.concatenate([taper[:, None] * jnp.cos(angle), -taper[:, None] * jnp.sin(angle)], axis=1)
    return table_full.astype(jnp.bfloat16)

def whiten(records, counts, gap_mask, fourier):
    channels, segments, samples = records.shape
    stations, hour_count = counts.shape
    seg_hour = segments // hour_count
    spectrum = jnp.dot(records.reshape(channels * segments, samples), fourier, preferred_element_type=jnp.float32).reshape(channels, segments, samples)
    band_power = lax.optimization_barrier(jnp.mean(spectrum * spectrum, axis=2, keepdims=True))
    position = jnp.arange(seg_hour, dtype=jnp.int32)
    station_valid = (position[None, None, :] < counts[:, :, None]).astype(jnp.float32)
    station_valid = station_valid * gap_mask.reshape(stations, hour_count, seg_hour).astype(jnp.float32)
    validity = jnp.repeat(station_valid.reshape(stations, segments), 3, axis=0)
    whitened = (spectrum * lax.rsqrt(band_power + epsilon) * validity[:, :, None]).astype(jnp.bfloat16)
    return (whitened.reshape(channels, hour_count, seg_hour, 2, samples // 2), validity.astype(jnp.bfloat16).reshape(channels, hour_count, seg_hour))

def pair_spectra(own_block, partner, own_valid, partner_valid):
    hour_count = own_block.shape[1]
    first = own_block.astype(jnp.float32)
    second = partner.astype(jnp.float32)
    real_part = jnp.einsum('ahspk,bhspk->hkab', first, second)
    imag_part = jnp.einsum('ahsk,bhsk->hkab', first[:, :, :, 1], second[:, :, :, 0]) - jnp.einsum('ahsk,bhsk->hkab', first[:, :, :, 0], second[:, :, :, 1])
    joint = jnp.einsum('ahs,bhs->hab', own_valid.astype(jnp.float32), partner_valid.astype(jnp.float32))
    weighting = 1.0 / (hour_count * jnp.maximum(joint, 1.0))
    real_sum = lax.optimization_barrier(jnp.sum(real_part * weighting[:, None], axis=0))
    imag_sum = lax.optimization_barrier(jnp.sum(imag_part * weighting[:, None], axis=0))
    return jnp.stack([jnp.transpose(real_sum, (1, 2, 0)), jnp.transpose(imag_sum, (1, 2, 0))]).astype(jnp.bfloat16)

def reference(records, counts, gap_mask):
    fourier = fourier_matrix(SEG_LEN)
    blocks_raw = records.reshape(N_STA, CH_DEV, SEGS, SEG_LEN)
    counts_blocks = counts.reshape(N_STA, ST_DEV, HOURS)
    gaps_blocks = gap_mask.reshape(N_STA, ST_DEV, SEGS)

    def prepare(pieces):
        return whiten(pieces[0], pieces[1], pieces[2], fourier)
    whitened, validity = lax.map(prepare, (blocks_raw, counts_blocks, gaps_blocks))

    def one_block(block_index):
        own_block = whitened[block_index]
        own_valid = validity[block_index]
        results = []
        for slot_index in range(2 * ROUNDS + 1):
            partner_idx = (block_index + slot_index - ROUNDS) % N_STA
            results.append(pair_spectra(own_block, whitened[partner_idx], own_valid, validity[partner_idx]))
        return jnp.stack(results)
    stacked = lax.map(one_block, jnp.arange(N_STA, dtype=jnp.int32))
    return jnp.transpose(stacked, (1, 2, 0, 3, 4, 5)).reshape(2 * ROUNDS + 1, 2, N_STA * CH_DEV, CH_DEV, F)
```

```python
import functools

import jax
import jax.numpy as jnp
import numpy as np
from jax import lax
from jax.experimental import pallas as pl
from jax.experimental.pallas import tpu as pltpu
from jax.sharding import PartitionSpec as P

ROUNDS = 3
TILE = 16
LANES = 128
EPSILON = 1e-06
NT = (((1,), (1,)), ((), ()))


def fourier_rows(samples):
    bins = samples // 2
    times = np.arange(samples, dtype=np.int32)
    phase = (times[:, None] * np.arange(bins, dtype=np.int32)[None, :]) % samples
    angle = np.float32(2.0 * np.pi / samples) * phase.astype(np.float32)
    half = times.astype(np.float32) + np.float32(0.5)
    taper = np.float32(0.5) - np.float32(0.5) * np.cos(np.float32(2.0 * np.pi / samples) * half)
    table = np.concatenate([taper[:, None] * np.cos(angle), -taper[:, None] * np.sin(angle)], axis=1)
    return jnp.asarray(np.ascontiguousarray(table.T), dtype=jnp.bfloat16)


def pick_rows(channels):
    out = np.zeros((2 * TILE, 2 * channels * TILE), np.float32)
    for part in range(2):
        for a in range(channels):
            start = (part * channels + a) * TILE
            out[part * TILE + a, start : start + TILE] = 1
    return jnp.asarray(out, dtype=jnp.bfloat16)


def spread_bins(channels, bins):
    row = np.arange(channels * TILE)
    col = np.arange(channels * bins)
    same = (row[:, None] // TILE == col[None, :] // bins) & (row[:, None] % TILE == col[None, :] % TILE)
    return jnp.asarray(same.astype(np.float32), dtype=jnp.bfloat16)


def kernel(
    dims, table, pick, spread, records, counts, gaps, lower, upper,
    own, turned, inbox, weights, gathered, outgoing, returned,
    send_sem, recv_sem, back_send, back_recv,
):
    channels, segments, samples, stations, hours, count = dims
    bins = samples // 2
    span = segments // hours
    groups = bins // TILE
    rows = channels * TILE
    per_station = channels // stations
    me = lax.axis_index("sta")
    kind = lax.rem(me, 4)
    core = lax.rem(kind, 2)
    side = kind // 2

    def at(offset):
        return lax.rem(me + offset + count, count)

    def barrier_signal():
        barrier = pltpu.get_barrier_semaphore()
        for offset in (1, 2, 3, 4, -1, -2, -3, -4):
            pl.semaphore_signal(
                barrier, inc=1, device_id={"sta": at(offset)}, device_id_type=pl.DeviceIdType.MESH
            )

    barrier_signal()

    position = lax.broadcasted_iota(jnp.int32, (stations, segments), 1)
    limit = jnp.zeros((stations, segments), jnp.int32)
    for h in range(hours):
        limit = jnp.where(position // span == h, counts[:, h : h + 1], limit)
    valid = jnp.where(lax.rem(position, span) < limit, gaps[...], 0).astype(jnp.float32)
    valid = jnp.concatenate(
        [jnp.broadcast_to(valid[s : s + 1], (per_station, segments)) for s in range(stations)]
        + [jnp.zeros((TILE - channels, segments), jnp.float32)],
        axis=0,
    )
    left = lax.broadcasted_iota(jnp.int32, (TILE, LANES), 1) < span
    for pair in range(hours // 2):
        block = valid[:, pair * LANES : (pair + 1) * LANES]
        first = jnp.where(left, block, 0.0)
        second = jnp.where(left, pltpu.roll(block, span, 1), 0.0)
        own[0, :, 2 * pair * LANES : (2 * pair + 1) * LANES] = first.astype(jnp.bfloat16)
        own[0, :, (2 * pair + 1) * LANES : (2 * pair + 2) * LANES] = second.astype(jnp.bfloat16)

    left_b = lax.broadcasted_iota(jnp.int32, (bins, LANES), 1) < span
    for c in range(channels):
        spectrum = lax.dot_general(table[...], records[c], NT, preferred_element_type=jnp.float32)
        power = jnp.sum(spectrum * spectrum, axis=0, keepdims=True) * (1.0 / samples)
        white = spectrum * (lax.rsqrt(power + EPSILON) * valid[c : c + 1])
        for pair in range(hours // 2):
            re = white[:bins, pair * LANES : (pair + 1) * LANES]
            im = white[bins:, pair * LANES : (pair + 1) * LANES]
            re_r = pltpu.roll(re, span, 1)
            im_r = pltpu.roll(im, span, 1)
            straight = (jnp.where(left_b, re, im_r), jnp.where(left_b, re_r, im))
            across = (jnp.where(left_b, im, -re_r), jnp.where(left_b, im_r, -re))
            for half in range(2):
                lanes = slice((2 * pair + half) * LANES, (2 * pair + half + 1) * LANES)
                flat = straight[half].astype(jnp.bfloat16)
                flat_t = across[half].astype(jnp.bfloat16)
                for g in range(groups):
                    own[1 + g * channels + c, :, lanes] = flat[g * TILE : (g + 1) * TILE]
                    turned[g * channels + c, :, lanes] = flat_t[g * TILE : (g + 1) * TILE]

    pl.semaphore_wait(pltpu.get_barrier_semaphore(), 8)

    def where_is(piece):
        if isinstance(piece, int) and piece == 0:
            return pl.ds(0, 1)
        return pl.ds(1 + (piece - 1) * channels, channels)

    def copy(source, piece, way, slot, target):
        return pltpu.make_async_remote_copy(
            src_ref=source.at[where_is(piece)],
            dst_ref=inbox.at[slot, where_is(piece)],
            send_sem=send_sem.at[way, piece],
            recv_sem=recv_sem.at[slot, piece],
            device_id={"sta": target},
            device_id_type=pl.DeviceIdType.MESH,
        )

    def ahead(piece):
        return copy(own, piece, 0, 1 + 2 * side, at(2 + 2 * side))

    def beside(piece):
        return copy(own, piece, 1, 2 * core, at(1 + 2 * core))

    def relay_twin(piece):
        return copy(inbox.at[1], piece, 2, 2 - 2 * core, at(1 - 2 * core))

    def relay_down(piece):
        return copy(inbox.at[3], piece, 3, 1, at(-2))

    def relay_twin_far(piece):
        return copy(inbox.at[3], piece, 1, 2, at(-1))

    def arrived(slot, piece):
        copy(own, piece, 0, slot, at(1)).wait_recv()

    def send_own(piece):
        ahead(piece).start()

        @pl.when(kind != 3)
        def _():
            beside(piece).start()

    def pass_on(piece):
        @pl.when(side == 1)
        def _():
            arrived(3, piece)
            relay_down(piece).start()

        @pl.when(kind == 3)
        def _():
            relay_twin_far(piece).start()

        arrived(1, piece)
        relay_twin(piece).start()

    send_own(0)
    for g in range(groups):
        send_own(1 + g)

    def dot_nt(a, b):
        return lax.dot_general(a, b, NT, preferred_element_type=jnp.float32)

    row_id = lax.broadcasted_iota(jnp.int32, (rows, rows), 0)
    col_id = lax.broadcasted_iota(jnp.int32, (rows, rows), 1)
    diagonal = lax.rem(row_id, TILE) == lax.rem(col_id, TILE)

    def widen(ref, h):
        block = ref[0, :, h * LANES : (h + 1) * LANES].astype(jnp.float32)
        return jnp.concatenate(
            [jnp.broadcast_to(block[c : c + 1], (TILE, LANES)) for c in range(channels)], axis=0
        ).astype(jnp.bfloat16)

    def weigh(d, partner):
        for h in range(hours):
            joint = dot_nt(widen(own, h), widen(partner, h))
            weights[d, h] = jnp.where(diagonal, 1.0 / (hours * jnp.maximum(joint, 1.0)), 0.0)

    lane_group = lax.rem(lax.broadcasted_iota(jnp.int32, (2 * TILE, channels * bins), 1), bins) // TILE

    def correlate(d, partner, g):
        at_rows = pl.ds(1 + g * channels, channels)
        t_rows = pl.ds(g * channels, channels)
        re = jnp.zeros((rows, rows), jnp.float32)
        im = jnp.zeros((rows, rows), jnp.float32)
        for h in range(hours):
            lanes = slice(h * LANES, (h + 1) * LANES)
            other = partner[at_rows, :, lanes].reshape(rows, LANES)
            mine = own[at_rows, :, lanes].reshape(rows, LANES)
            mine_t = turned[t_rows, :, lanes].reshape(rows, LANES)
            scale = weights[d, h]
            re = re + dot_nt(mine, other) * scale
            im = im + dot_nt(mine_t, other) * scale
        both = jnp.concatenate([re, im], axis=0).astype(jnp.bfloat16)
        picked = jnp.dot(pick[...], both, preferred_element_type=jnp.float32).astype(jnp.bfloat16)
        wide = jnp.dot(picked, spread[...], preferred_element_type=jnp.float32)
        gathered[d] = jnp.where(lane_group == g, wide, gathered[d])

    gathered[...] = jnp.zeros_like(gathered)
    weigh(0, own)

    @pl.loop(0, groups)
    def _(g):
        correlate(0, own, g)

    pass_on(0)
    arrived(0, 0)
    arrived(2, 0)
    for d in range(1, ROUNDS + 1):
        weigh(d, inbox.at[d - 1])

    @pl.loop(0, groups)
    def _(g):
        pass_on(g + 1)
        arrived(0, g + 1)
        arrived(2, g + 1)
        for d in range(1, ROUNDS + 1):
            correlate(d, inbox.at[d - 1], g)

    def give_back(d):
        return pltpu.make_async_remote_copy(
            src_ref=outgoing.at[d - 1],
            dst_ref=returned.at[d - 1],
            send_sem=back_send.at[d - 1],
            recv_sem=back_recv.at[d - 1],
            device_id={"sta": at(-d)},
            device_id_type=pl.DeviceIdType.MESH,
        )

    for d in range(ROUNDS, 0, -1):
        for part in range(2):
            for b in range(channels):
                value = gathered[d, part * TILE : (part + 1) * TILE, b * bins : (b + 1) * bins]
                outgoing[d - 1, part, b] = (value if part == 0 else -value).astype(jnp.bfloat16)
        give_back(d).start()
    for d in range(ROUNDS + 1):
        for part in range(2):
            for b in range(channels):
                value = gathered[d, part * TILE : (part + 1) * TILE, b * bins : (b + 1) * bins]
                lower[ROUNDS - d, part, b] = value.astype(jnp.bfloat16)

    for piece in range(groups + 1):
        ahead(piece).wait_send()
        beside(piece).wait_send()
        relay_twin(piece).wait_send()

        @pl.when(side == 1)
        def _():
            relay_down(piece).wait_send()

    for d in range(ROUNDS, 0, -1):
        give_back(d).wait()
    upper[...] = returned[...]


def per_device(count, records, counts, gap_mask):
    channels, segments, samples = records.shape
    stations, hours = counts.shape
    bins = samples // 2
    groups = bins // TILE
    rows = channels * TILE
    blocks = 1 + groups * channels
    wide = hours * LANES
    dims = (channels, segments, samples, stations, hours, count)
    vmem = pl.BlockSpec(memory_space=pltpu.VMEM)
    lower, upper = pl.pallas_call(
        functools.partial(kernel, dims),
        out_shape=(
            jax.ShapeDtypeStruct((ROUNDS + 1, 2, channels, TILE, bins), jnp.bfloat16),
            jax.ShapeDtypeStruct((ROUNDS, 2, channels, TILE, bins), jnp.bfloat16),
        ),
        in_specs=[vmem] * 6,
        out_specs=(vmem, vmem),
        scratch_shapes=[
            pltpu.VMEM((blocks, TILE, wide), jnp.bfloat16),
            pltpu.VMEM((blocks - 1, TILE, wide), jnp.bfloat16),
            pltpu.VMEM((ROUNDS + 1, blocks, TILE, wide), jnp.bfloat16),
            pltpu.VMEM((ROUNDS + 1, hours, rows, rows), jnp.float32),
            pltpu.VMEM((ROUNDS + 1, 2 * TILE, channels * bins), jnp.float32),
            pltpu.VMEM((ROUNDS, 2, channels, TILE, bins), jnp.bfloat16),
            pltpu.VMEM((ROUNDS, 2, channels, TILE, bins), jnp.bfloat16),
            pltpu.SemaphoreType.DMA((4, groups + 1)),
            pltpu.SemaphoreType.DMA((4, groups + 1)),
            pltpu.SemaphoreType.DMA((ROUNDS,)),
            pltpu.SemaphoreType.DMA((ROUNDS,)),
        ],
        compiler_params=pltpu.CompilerParams(
            collective_id=0, has_side_effects=True, vmem_limit_bytes=48 * 1024 * 1024
        ),
    )(
        fourier_rows(samples), pick_rows(channels), spread_bins(channels, bins),
        records, counts, gap_mask,
    )
    below = jnp.transpose(lower[:, :, :, :channels], (0, 1, 3, 2, 4))
    return jnp.concatenate([below, upper[:, :, :, :channels]], axis=0)


def solution(mesh):
    count = mesh.shape["sta"]
    return jax.shard_map(
        functools.partial(per_device, count),
        mesh=mesh,
        in_specs=(P(("days", "sta"), None, None), P(("days", "sta"), None), P(("days", "sta"), None)),
        out_specs=P(None, None, ("days", "sta"), None, None),
        check_vma=False,
    )
```

```python
import functools

import jax
import jax.numpy as jnp
import numpy as np
from jax import lax
from jax.experimental import pallas as pl
from jax.experimental.pallas import tpu as pltpu
from jax.sharding import PartitionSpec as P

ROUNDS = 3
TILE = 16
LANES = 128
PARTS = 2
LAG = 2
EPSILON = 1e-06
NT = (((1,), (1,)), ((), ()))


def fourier_rows(samples):
    bins = samples // 2
    times = np.arange(samples, dtype=np.int32)
    phase = (times[:, None] * np.arange(bins, dtype=np.int32)[None, :]) % samples
    angle = np.float32(2.0 * np.pi / samples) * phase.astype(np.float32)
    half = times.astype(np.float32) + np.float32(0.5)
    taper = np.float32(0.5) - np.float32(0.5) * np.cos(np.float32(2.0 * np.pi / samples) * half)
    table = np.concatenate([taper[:, None] * np.cos(angle), -taper[:, None] * np.sin(angle)], axis=1)
    return jnp.asarray(np.ascontiguousarray(table.T), dtype=jnp.bfloat16)


def pick_rows(channels):
    out = np.zeros((2 * TILE, 2 * channels * TILE), np.float32)
    for part in range(2):
        for a in range(channels):
            start = (part * channels + a) * TILE
            out[part * TILE + a, start : start + TILE] = 1
    return jnp.asarray(out, dtype=jnp.bfloat16)


def spread_bins(channels, bins):
    row = np.arange(channels * TILE)
    col = np.arange(channels * bins)
    same = (row[:, None] // TILE == col[None, :] // bins) & (row[:, None] % TILE == col[None, :] % TILE)
    return jnp.asarray(same.astype(np.float32), dtype=jnp.bfloat16)


def kernel(
    dims, table_in, pick_in, spread_in, records_in, counts_in, gaps_in, result,
    table, pick, spread, records, counts, gaps,
    own, turned, inbox, weights, gathered, outgoing, returned,
    load_sem, send_sem, recv_sem, back_send, back_recv,
):
    channels, segments, samples, stations, hours, count = dims
    bins = samples // 2
    span = segments // hours
    groups = bins // TILE
    rows = channels * TILE
    per_station = channels // stations
    me = lax.axis_index("sta")
    kind = lax.rem(me, 4)
    core = lax.rem(kind, 2)
    side = kind // 2

    def at(offset):
        return lax.rem(me + offset + count, count)

    def barrier_signal():
        barrier = pltpu.get_barrier_semaphore()
        for offset in (1, 2, 3, 4, -1, -2, -3, -4):
            pl.semaphore_signal(
                barrier, inc=1, device_id={"sta": at(offset)}, device_id_type=pl.DeviceIdType.MESH
            )

    loads = [
        pltpu.make_async_copy(source, target, load_sem.at[i])
        for i, (source, target) in enumerate(
            (
                (table_in, table), (counts_in, counts), (gaps_in, gaps),
                (pick_in, pick), (spread_in, spread),
            )
        )
    ]
    for load in loads:
        load.start()
    record_loads = [
        pltpu.make_async_copy(records_in.at[c], records.at[c], load_sem.at[len(loads) + c])
        for c in range(channels)
    ]
    for load in record_loads:
        load.start()
    barrier_signal()
    gathered[...] = jnp.zeros_like(gathered)
    for load in loads:
        load.wait()

    position = lax.broadcasted_iota(jnp.int32, (stations, segments), 1)
    limit = jnp.zeros((stations, segments), jnp.int32)
    for h in range(hours):
        limit = jnp.where(position // span == h, counts[:, h : h + 1], limit)
    valid = jnp.where(lax.rem(position, span) < limit, gaps[...], 0).astype(jnp.float32)
    valid = jnp.concatenate(
        [jnp.broadcast_to(valid[s : s + 1], (per_station, segments)) for s in range(stations)]
        + [jnp.zeros((TILE - channels, segments), jnp.float32)],
        axis=0,
    )
    left = lax.broadcasted_iota(jnp.int32, (TILE, LANES), 1) < span
    for pair in range(hours // 2):
        block = valid[:, pair * LANES : (pair + 1) * LANES]
        first = jnp.where(left, block, 0.0)
        second = jnp.where(left, pltpu.roll(block, span, 1), 0.0)
        own[0, :, 2 * pair * LANES : (2 * pair + 1) * LANES] = first.astype(jnp.bfloat16)
        own[0, :, (2 * pair + 1) * LANES : (2 * pair + 2) * LANES] = second.astype(jnp.bfloat16)

    left_b = lax.broadcasted_iota(jnp.int32, (bins, LANES), 1) < span
    for c in range(channels):
        record_loads[c].wait()
        spectrum = lax.dot_general(table[...], records[c], NT, preferred_element_type=jnp.float32)
        power = jnp.sum(spectrum * spectrum, axis=0, keepdims=True) * (1.0 / samples)
        white = spectrum * (lax.rsqrt(power + EPSILON) * valid[c : c + 1])
        for pair in range(hours // 2):
            re = white[:bins, pair * LANES : (pair + 1) * LANES]
            im = white[bins:, pair * LANES : (pair + 1) * LANES]
            re_r = pltpu.roll(re, span, 1)
            im_r = pltpu.roll(im, span, 1)
            straight = (jnp.where(left_b, re, im_r), jnp.where(left_b, re_r, im))
            across = (jnp.where(left_b, im, -re_r), jnp.where(left_b, im_r, -re))
            for half in range(2):
                lanes = slice((2 * pair + half) * LANES, (2 * pair + half + 1) * LANES)
                flat = straight[half].astype(jnp.bfloat16)
                flat_t = across[half].astype(jnp.bfloat16)
                for g in range(groups):
                    own[1 + g * channels + c, :, lanes] = flat[g * TILE : (g + 1) * TILE]
                    turned[g * channels + c, :, lanes] = flat_t[g * TILE : (g + 1) * TILE]

    pl.semaphore_wait(pltpu.get_barrier_semaphore(), 8)

    part_rows = channels // PARTS

    def where_is(piece):
        if isinstance(piece, int) and piece == 0:
            return pl.ds(0, 1)
        return pl.ds(1 + (piece - 1) * part_rows, part_rows)

    def copy(source, piece, way, slot, target):
        return pltpu.make_async_remote_copy(
            src_ref=source.at[where_is(piece)],
            dst_ref=inbox.at[slot, where_is(piece)],
            send_sem=send_sem.at[way, piece],
            recv_sem=recv_sem.at[slot, piece],
            device_id={"sta": target},
            device_id_type=pl.DeviceIdType.MESH,
        )

    def ahead(piece):
        return copy(own, piece, 0, 1 + 2 * side, at(2 + 2 * side))

    def beside(piece):
        return copy(own, piece, 1, 2 * core, at(1 + 2 * core))

    def relay_twin(piece):
        return copy(inbox.at[1], piece, 2, 2 - 2 * core, at(1 - 2 * core))

    def relay_down(piece):
        return copy(inbox.at[3], piece, 3, 1, at(-2))

    def relay_twin_far(piece):
        return copy(inbox.at[3], piece, 1, 2, at(-1))

    def arrived(slot, piece):
        copy(own, piece, 0, slot, at(1)).wait_recv()

    def send_own(piece):
        ahead(piece).start()

        @pl.when(kind != 3)
        def _():
            beside(piece).start()

    def pass_on(piece):
        @pl.when(side == 1)
        def _():
            arrived(3, piece)
            relay_down(piece).start()

        @pl.when(kind == 3)
        def _():
            relay_twin_far(piece).start()

        arrived(1, piece)
        relay_twin(piece).start()

    send_own(0)
    for piece in range(groups * PARTS):
        send_own(1 + piece)

    def dot_nt(a, b):
        return lax.dot_general(a, b, NT, preferred_element_type=jnp.float32)

    row_id = lax.broadcasted_iota(jnp.int32, (rows, rows), 0)
    col_id = lax.broadcasted_iota(jnp.int32, (rows, rows), 1)
    diagonal = lax.rem(row_id, TILE) == lax.rem(col_id, TILE)

    def widen(ref, h):
        block = ref[0, :, h * LANES : (h + 1) * LANES].astype(jnp.float32)
        return jnp.concatenate(
            [jnp.broadcast_to(block[c : c + 1], (TILE, LANES)) for c in range(channels)], axis=0
        ).astype(jnp.bfloat16)

    def weigh(d, partner):
        for h in range(hours):
            joint = dot_nt(widen(own, h), widen(partner, h))
            weights[d, h] = jnp.where(diagonal, 1.0 / (hours * jnp.maximum(joint, 1.0)), 0.0)

    lane_group = lax.rem(lax.broadcasted_iota(jnp.int32, (2 * TILE, channels * bins), 1), bins) // TILE

    def correlate(d, partner, g):
        at_rows = pl.ds(1 + g * channels, channels)
        t_rows = pl.ds(g * channels, channels)
        re = jnp.zeros((rows, rows), jnp.float32)
        im = jnp.zeros((rows, rows), jnp.float32)
        for h in range(hours):
            lanes = slice(h * LANES, (h + 1) * LANES)
            other = partner[at_rows, :, lanes].reshape(rows, LANES)
            mine = own[at_rows, :, lanes].reshape(rows, LANES)
            mine_t = turned[t_rows, :, lanes].reshape(rows, LANES)
            scale = weights[d, h]
            re = re + dot_nt(mine, other) * scale
            im = im + dot_nt(mine_t, other) * scale
        both = jnp.concatenate([re, im], axis=0).astype(jnp.bfloat16)
        return jnp.dot(pick[...], both, preferred_element_type=jnp.float32).astype(jnp.bfloat16)

    def give_back(d, g):
        return pltpu.make_async_remote_copy(
            src_ref=outgoing.at[d - 1, g],
            dst_ref=returned.at[d - 1, g],
            send_sem=back_send.at[d - 1, g],
            recv_sem=back_recv.at[d - 1, g],
            device_id={"sta": at(-d)},
            device_id_type=pl.DeviceIdType.MESH,
        )

    def place(first, picked, g):
        wide = jnp.dot(
            jnp.concatenate(picked, axis=0), spread[...], preferred_element_type=jnp.float32
        )
        for i in range(len(picked)):
            rows_i = wide[i * 2 * TILE : (i + 1) * 2 * TILE]
            gathered[first + i] = jnp.where(lane_group == g, rows_i, gathered[first + i])

    def take_back(g):
        for d in range(1, ROUNDS + 1):
            give_back(d, g).wait_recv()
        place(ROUNDS + 1, [returned[d - 1, g] for d in range(1, ROUNDS + 1)], g)

    weigh(0, own)
    pass_on(0)
    arrived(0, 0)
    arrived(2, 0)
    for d in range(1, ROUNDS + 1):
        weigh(d, inbox.at[d - 1])

    @pl.loop(0, groups)
    def _(g):
        pieces = [1 + g * PARTS + part for part in range(PARTS)]
        pass_on(pieces[0])
        picked = [correlate(0, own, g)]
        for piece in pieces[1:]:
            pass_on(piece)
        for piece in pieces:
            arrived(0, piece)
            arrived(2, piece)
        for d in range(1, ROUNDS + 1):
            picked.append(correlate(d, inbox.at[d - 1], g))
            outgoing[d - 1, g] = picked[d]
            give_back(d, g).start()
        place(0, picked, g)

        @pl.when(g >= LAG)
        def _():
            take_back(g - LAG)

    for g in range(groups - LAG, groups):
        take_back(g)

    for q in range(2 * ROUNDS + 1):
        d = ROUNDS - q if q <= ROUNDS else q
        for part in range(2):
            for b in range(channels):
                value = gathered[d, part * TILE : (part + 1) * TILE, b * bins : (b + 1) * bins]
                if q > ROUNDS and part == 1:
                    value = -value
                result[q, part, b] = value.astype(jnp.bfloat16)

    @pl.loop(0, groups)
    def _(g):
        for d in range(1, ROUNDS + 1):
            give_back(d, g).wait_send()

    def sent(piece):
        ahead(piece).wait_send()
        beside(piece).wait_send()
        relay_twin(piece).wait_send()

        @pl.when(side == 1)
        def _():
            relay_down(piece).wait_send()

    sent(0)

    @pl.loop(0, groups * PARTS)
    def _(i):
        sent(i + 1)


def per_device(count, records, counts, gap_mask):
    channels, segments, samples = records.shape
    stations, hours = counts.shape
    bins = samples // 2
    groups = bins // TILE
    rows = channels * TILE
    blocks = 1 + groups * channels
    wide = hours * LANES
    dims = (channels, segments, samples, stations, hours, count)
    pieces = groups * PARTS + 1
    result = pl.pallas_call(
        functools.partial(kernel, dims),
        out_shape=jax.ShapeDtypeStruct((2 * ROUNDS + 1, 2, channels, TILE, bins), jnp.bfloat16),
        in_specs=[pl.BlockSpec(memory_space=pl.ANY)] * 6,
        out_specs=pl.BlockSpec(memory_space=pltpu.VMEM),
        scratch_shapes=[
            pltpu.VMEM((samples, samples), jnp.bfloat16),
            pltpu.VMEM((2 * TILE, 2 * rows), jnp.bfloat16),
            pltpu.VMEM((rows, channels * bins), jnp.bfloat16),
            pltpu.VMEM((channels, segments, samples), jnp.bfloat16),
            pltpu.VMEM((stations, hours), jnp.int32),
            pltpu.VMEM((stations, segments), jnp.int32),
            pltpu.VMEM((blocks, TILE, wide), jnp.bfloat16),
            pltpu.VMEM((blocks - 1, TILE, wide), jnp.bfloat16),
            pltpu.VMEM((ROUNDS + 1, blocks, TILE, wide), jnp.bfloat16),
            pltpu.VMEM((ROUNDS + 1, hours, rows, rows), jnp.float32),
            pltpu.VMEM((2 * ROUNDS + 1, 2 * TILE, channels * bins), jnp.float32),
            pltpu.VMEM((ROUNDS, groups, 2 * TILE, rows), jnp.bfloat16),
            pltpu.VMEM((ROUNDS, groups, 2 * TILE, rows), jnp.bfloat16),
            pltpu.SemaphoreType.DMA((5 + channels,)),
            pltpu.SemaphoreType.DMA((4, pieces)),
            pltpu.SemaphoreType.DMA((4, pieces)),
            pltpu.SemaphoreType.DMA((ROUNDS, groups)),
            pltpu.SemaphoreType.DMA((ROUNDS, groups)),
        ],
        compiler_params=pltpu.CompilerParams(
            collective_id=0, has_side_effects=True, vmem_limit_bytes=60 * 1024 * 1024
        ),
    )(
        fourier_rows(samples), pick_rows(channels), spread_bins(channels, bins),
        records, counts, gap_mask,
    )
    result = result[:, :, :, :channels]
    below = jnp.transpose(result[: ROUNDS + 1], (0, 1, 3, 2, 4))
    return jnp.concatenate([below, result[ROUNDS + 1 :]], axis=0)


def solution(mesh):
    count = mesh.shape["sta"]
    return jax.shard_map(
        functools.partial(per_device, count),
        mesh=mesh,
        in_specs=(P(("days", "sta"), None, None), P(("days", "sta"), None), P(("days", "sta"), None)),
        out_specs=P(None, None, ("days", "sta"), None, None),
        check_vma=False,
    )
```

```python
import functools

import jax
import jax.numpy as jnp
import numpy as np
from jax import lax
from jax.experimental import pallas as pl
from jax.experimental.pallas import tpu as pltpu
from jax.sharding import PartitionSpec as P

ROUNDS = 3
TILE = 16
LANES = 128
PARTS = 2
LAG = 2
COLS = 256
EPSILON = 1e-06
NT = (((1,), (1,)), ((), ()))


def fourier_rows(samples):
    bins = samples // 2
    times = np.arange(samples, dtype=np.int32)
    phase = (times[:, None] * np.arange(bins, dtype=np.int32)[None, :]) % samples
    angle = np.float32(2.0 * np.pi / samples) * phase.astype(np.float32)
    half = times.astype(np.float32) + np.float32(0.5)
    taper = np.float32(0.5) - np.float32(0.5) * np.cos(np.float32(2.0 * np.pi / samples) * half)
    table = np.concatenate([taper[:, None] * np.cos(angle), -taper[:, None] * np.sin(angle)], axis=1)
    return jnp.asarray(np.ascontiguousarray(table.T), dtype=jnp.bfloat16)


def pick_rows(channels):
    out = np.zeros((2 * TILE, 2 * channels * TILE), np.float32)
    for part in range(2):
        for a in range(channels):
            start = (part * channels + a) * TILE
            out[part * TILE + a, start : start + TILE] = 1
    return jnp.asarray(out, dtype=jnp.bfloat16)


def spread_bins(channels, bins):
    row = np.arange(channels * TILE)
    col = np.arange(channels * bins)
    same = (row[:, None] // TILE == col[None, :] // bins) & (row[:, None] % TILE == col[None, :] % TILE)
    return jnp.asarray(same.astype(np.float32), dtype=jnp.bfloat16)


def kernel(
    dims, table_in, pick_in, spread_in, records_in, counts_in, gaps_in, result,
    table, pick, spread, records, counts, gaps,
    own, turned, inbox, weights, gathered, selves, outgoing, returned,
    load_sem, send_sem, recv_sem, back_send, back_recv,
):
    channels, segments, samples, stations, hours, count = dims
    bins = samples // 2
    span = segments // hours
    groups = bins // TILE
    rows = channels * TILE
    per_station = channels // stations
    me = lax.axis_index("sta")
    kind = lax.rem(me, 4)
    core = lax.rem(kind, 2)
    side = kind // 2

    def at(offset):
        return lax.rem(me + offset + count, count)

    def barrier_signal():
        barrier = pltpu.get_barrier_semaphore()
        for offset in (1, 2, 3, 4, -1, -2, -3, -4):
            pl.semaphore_signal(
                barrier, inc=1, device_id={"sta": at(offset)}, device_id_type=pl.DeviceIdType.MESH
            )

    loads = [
        pltpu.make_async_copy(source, target, load_sem.at[i])
        for i, (source, target) in enumerate(
            (
                (table_in, table), (counts_in, counts), (gaps_in, gaps),
                (pick_in, pick), (spread_in, spread),
            )
        )
    ]
    for load in loads:
        load.start()
    record_loads = [
        pltpu.make_async_copy(records_in.at[c], records.at[c], load_sem.at[len(loads) + c])
        for c in range(channels)
    ]
    for load in record_loads:
        load.start()
    barrier_signal()
    gathered[...] = jnp.zeros_like(gathered)
    for load in loads:
        load.wait()

    position = lax.broadcasted_iota(jnp.int32, (stations, segments), 1)
    limit = jnp.zeros((stations, segments), jnp.int32)
    for h in range(hours):
        limit = jnp.where(position // span == h, counts[:, h : h + 1], limit)
    valid = jnp.where(lax.rem(position, span) < limit, gaps[...], 0).astype(jnp.float32)
    valid = jnp.concatenate(
        [jnp.broadcast_to(valid[s : s + 1], (per_station, segments)) for s in range(stations)]
        + [jnp.zeros((TILE - channels, segments), jnp.float32)],
        axis=0,
    )
    left = lax.broadcasted_iota(jnp.int32, (TILE, LANES), 1) < span
    for pair in range(hours // 2):
        block = valid[:, pair * LANES : (pair + 1) * LANES]
        first = jnp.where(left, block, 0.0)
        second = jnp.where(left, pltpu.roll(block, span, 1), 0.0)
        own[0, :, 2 * pair * LANES : (2 * pair + 1) * LANES] = first.astype(jnp.bfloat16)
        own[0, :, (2 * pair + 1) * LANES : (2 * pair + 2) * LANES] = second.astype(jnp.bfloat16)

    left_b = lax.broadcasted_iota(jnp.int32, (bins, LANES), 1) < span
    for c in range(channels):
        record_loads[c].wait()
        spectrum = lax.dot_general(table[...], records[c], NT, preferred_element_type=jnp.float32)
        power = jnp.sum(spectrum * spectrum, axis=0, keepdims=True) * (1.0 / samples)
        white = spectrum * (lax.rsqrt(power + EPSILON) * valid[c : c + 1])
        for pair in range(hours // 2):
            re = white[:bins, pair * LANES : (pair + 1) * LANES]
            im = white[bins:, pair * LANES : (pair + 1) * LANES]
            re_r = pltpu.roll(re, span, 1)
            im_r = pltpu.roll(im, span, 1)
            straight = (jnp.where(left_b, re, im_r), jnp.where(left_b, re_r, im))
            across = (jnp.where(left_b, im, -re_r), jnp.where(left_b, im_r, -re))
            for half in range(2):
                lanes = slice((2 * pair + half) * LANES, (2 * pair + half + 1) * LANES)
                flat = straight[half].astype(jnp.bfloat16)
                flat_t = across[half].astype(jnp.bfloat16)
                for g in range(groups):
                    own[1 + g * channels + c, :, lanes] = flat[g * TILE : (g + 1) * TILE]
                    turned[g * channels + c, :, lanes] = flat_t[g * TILE : (g + 1) * TILE]

    pl.semaphore_wait(pltpu.get_barrier_semaphore(), 8)

    part_rows = channels // PARTS

    def where_is(piece):
        if isinstance(piece, int) and piece == 0:
            return pl.ds(0, 1)
        return pl.ds(1 + (piece - 1) * part_rows, part_rows)

    def copy(source, piece, way, slot, target):
        return pltpu.make_async_remote_copy(
            src_ref=source.at[where_is(piece)],
            dst_ref=inbox.at[slot, where_is(piece)],
            send_sem=send_sem.at[way, piece],
            recv_sem=recv_sem.at[slot, piece],
            device_id={"sta": target},
            device_id_type=pl.DeviceIdType.MESH,
        )

    def ahead(piece):
        return copy(own, piece, 0, 1 + 2 * side, at(2 + 2 * side))

    def beside(piece):
        return copy(own, piece, 1, 2 * core, at(1 + 2 * core))

    def relay_twin(piece):
        return copy(inbox.at[1], piece, 2, 2 - 2 * core, at(1 - 2 * core))

    def relay_down(piece):
        return copy(inbox.at[3], piece, 3, 1, at(-2))

    def relay_twin_far(piece):
        return copy(inbox.at[3], piece, 1, 2, at(-1))

    def arrived(slot, piece):
        copy(own, piece, 0, slot, at(1)).wait_recv()

    def send_own(piece):
        ahead(piece).start()

        @pl.when(kind != 3)
        def _():
            beside(piece).start()

    def pass_on(piece):
        @pl.when(side == 1)
        def _():
            arrived(3, piece)
            relay_down(piece).start()

        @pl.when(kind == 3)
        def _():
            relay_twin_far(piece).start()

        arrived(1, piece)
        relay_twin(piece).start()

    send_own(0)
    for piece in range(groups * PARTS):
        send_own(1 + piece)

    def dot_nt(a, b):
        return lax.dot_general(a, b, NT, preferred_element_type=jnp.float32)

    partners = (own,) + tuple(inbox.at[d] for d in range(ROUNDS))
    chunks = (ROUNDS + 1) * rows // COLS
    each = COLS // TILE

    def columns(blocks, n):
        out = []
        for d, block in enumerate(blocks):
            first = max(each * n, d * channels) - d * channels
            last = min(each * (n + 1), (d + 1) * channels) - d * channels
            if first < last:
                out.append(block[first * TILE : last * TILE])
        return jnp.concatenate(out, axis=0) if len(out) > 1 else out[0]

    def widen(ref, h):
        block = ref[0, :, h * LANES : (h + 1) * LANES].astype(jnp.float32)
        return jnp.concatenate(
            [jnp.broadcast_to(block[c : c + 1], (TILE, LANES)) for c in range(channels)], axis=0
        ).astype(jnp.bfloat16)

    def weigh():
        row_id = lax.broadcasted_iota(jnp.int32, (rows, COLS), 0)
        col_id = lax.broadcasted_iota(jnp.int32, (rows, COLS), 1)
        diagonal = lax.rem(row_id, TILE) == lax.rem(col_id, TILE)
        for h in range(hours):
            wide = [widen(ref, h) for ref in partners]
            for n in range(chunks):
                joint = dot_nt(wide[0], columns(wide, n))
                weights[h, n] = jnp.where(diagonal, 1.0 / (hours * jnp.maximum(joint, 1.0)), 0.0)

    lane_group = lax.rem(lax.broadcasted_iota(jnp.int32, (2 * TILE, channels * bins), 1), bins) // TILE

    def correlate(g):
        at_rows = pl.ds(1 + g * channels, channels)
        t_rows = pl.ds(g * channels, channels)
        picked = []
        for n in range(chunks):
            re = jnp.zeros((rows, COLS), jnp.float32)
            im = jnp.zeros((rows, COLS), jnp.float32)
            for h in range(hours):
                lanes = slice(h * LANES, (h + 1) * LANES)
                blocks = [ref[at_rows, :, lanes].reshape(rows, LANES) for ref in partners]
                mine_t = turned[t_rows, :, lanes].reshape(rows, LANES)
                product = dot_nt(jnp.concatenate([blocks[0], mine_t], axis=0), columns(blocks, n))
                scale = weights[h, n]
                re = re + product[:rows] * scale
                im = im + product[rows:] * scale
            both = jnp.concatenate([re, im], axis=0).astype(jnp.bfloat16)
            picked.append(jnp.dot(pick[...], both, preferred_element_type=jnp.float32))
        return jnp.concatenate(picked, axis=1)

    def give_back(d, g):
        return pltpu.make_async_remote_copy(
            src_ref=outgoing.at[d - 1, g],
            dst_ref=returned.at[d - 1, g],
            send_sem=back_send.at[d - 1, g],
            recv_sem=back_recv.at[d - 1, g],
            device_id={"sta": at(-d)},
            device_id_type=pl.DeviceIdType.MESH,
        )

    def place(g):
        for d in range(1, ROUNDS + 1):
            give_back(d, g).wait_recv()
        parts = [selves[g]]
        parts += [outgoing[d, g] for d in range(ROUNDS)]
        parts += [returned[d, g] for d in range(ROUNDS)]
        wide = jnp.dot(
            jnp.concatenate(parts, axis=0), spread[...], preferred_element_type=jnp.float32
        )
        for i in range(len(parts)):
            rows_i = wide[i * 2 * TILE : (i + 1) * 2 * TILE]
            gathered[i] = jnp.where(lane_group == g, rows_i, gathered[i])

    pass_on(0)
    arrived(0, 0)
    arrived(2, 0)
    weigh()

    @pl.loop(0, groups)
    def _(g):
        pieces = [1 + g * PARTS + part for part in range(PARTS)]
        for piece in pieces:
            pass_on(piece)
        for piece in pieces:
            arrived(0, piece)
            arrived(2, piece)
        picked = correlate(g)
        for d in range(1, ROUNDS + 1):
            outgoing[d - 1, g] = picked[:, d * rows : (d + 1) * rows].astype(jnp.bfloat16)
            give_back(d, g).start()
        selves[g] = picked[:, :rows].astype(jnp.bfloat16)

        @pl.when(g >= LAG)
        def _():
            place(g - LAG)

    for g in range(groups - LAG, groups):
        place(g)

    for q in range(2 * ROUNDS + 1):
        d = ROUNDS - q if q <= ROUNDS else q
        for part in range(2):
            for b in range(channels):
                value = gathered[d, part * TILE : (part + 1) * TILE, b * bins : (b + 1) * bins]
                if q > ROUNDS and part == 1:
                    value = -value
                result[q, part, b] = value.astype(jnp.bfloat16)

    @pl.loop(0, groups)
    def _(g):
        for d in range(1, ROUNDS + 1):
            give_back(d, g).wait_send()

    def sent(piece):
        ahead(piece).wait_send()
        beside(piece).wait_send()
        relay_twin(piece).wait_send()

        @pl.when(side == 1)
        def _():
            relay_down(piece).wait_send()

    sent(0)

    @pl.loop(0, groups * PARTS)
    def _(i):
        sent(i + 1)


def per_device(count, records, counts, gap_mask):
    channels, segments, samples = records.shape
    stations, hours = counts.shape
    bins = samples // 2
    groups = bins // TILE
    rows = channels * TILE
    blocks = 1 + groups * channels
    wide = hours * LANES
    dims = (channels, segments, samples, stations, hours, count)
    pieces = groups * PARTS + 1
    result = pl.pallas_call(
        functools.partial(kernel, dims),
        out_shape=jax.ShapeDtypeStruct((2 * ROUNDS + 1, 2, channels, TILE, bins), jnp.bfloat16),
        in_specs=[pl.BlockSpec(memory_space=pltpu.HBM)] * 6,
        out_specs=pl.BlockSpec(memory_space=pltpu.VMEM),
        scratch_shapes=[
            pltpu.VMEM((samples, samples), jnp.bfloat16),
            pltpu.VMEM((2 * TILE, 2 * rows), jnp.bfloat16),
            pltpu.VMEM((rows, channels * bins), jnp.bfloat16),
            pltpu.VMEM((channels, segments, samples), jnp.bfloat16),
            pltpu.VMEM((stations, hours), jnp.int32),
            pltpu.VMEM((stations, segments), jnp.int32),
            pltpu.VMEM((blocks, TILE, wide), jnp.bfloat16),
            pltpu.VMEM((blocks - 1, TILE, wide), jnp.bfloat16),
            pltpu.VMEM((ROUNDS + 1, blocks, TILE, wide), jnp.bfloat16),
            pltpu.VMEM((hours, (ROUNDS + 1) * rows // COLS, rows, COLS), jnp.float32),
            pltpu.VMEM((2 * ROUNDS + 1, 2 * TILE, channels * bins), jnp.float32),
            pltpu.VMEM((groups, 2 * TILE, rows), jnp.bfloat16),
            pltpu.VMEM((ROUNDS, groups, 2 * TILE, rows), jnp.bfloat16),
            pltpu.VMEM((ROUNDS, groups, 2 * TILE, rows), jnp.bfloat16),
            pltpu.SemaphoreType.DMA((5 + channels,)),
            pltpu.SemaphoreType.DMA((4, pieces)),
            pltpu.SemaphoreType.DMA((4, pieces)),
            pltpu.SemaphoreType.DMA((ROUNDS, groups)),
            pltpu.SemaphoreType.DMA((ROUNDS, groups)),
        ],
        compiler_params=pltpu.CompilerParams(
            collective_id=0, has_side_effects=True, vmem_limit_bytes=54 * 1024 * 1024
        ),
    )(
        fourier_rows(samples), pick_rows(channels), spread_bins(channels, bins),
        records, counts, gap_mask,
    )
    result = result[:, :, :, :channels]
    below = jnp.transpose(result[: ROUNDS + 1], (0, 1, 3, 2, 4))
    return jnp.concatenate([below, result[ROUNDS + 1 :]], axis=0)


def solution(mesh):
    count = mesh.shape["sta"]
    return jax.shard_map(
        functools.partial(per_device, count),
        mesh=mesh,
        in_specs=(P(("days", "sta"), None, None), P(("days", "sta"), None), P(("days", "sta"), None)),
        out_specs=P(None, None, ("days", "sta"), None, None),
        check_vma=False,
    )
```

```python
import functools

import jax
import jax.numpy as jnp
import numpy as np
from jax import lax
from jax.experimental import pallas as pl
from jax.experimental.pallas import tpu as pltpu
from jax.sharding import PartitionSpec as P

ROUNDS = 3
TILE = 16
LANES = 128
PARTS = 1
COLS = 256
EPSILON = 1e-06
NT = (((1,), (1,)), ((), ()))


def fourier_rows(samples):
    bins = samples // 2
    times = np.arange(samples, dtype=np.int32)
    phase = (times[:, None] * np.arange(bins, dtype=np.int32)[None, :]) % samples
    angle = np.float32(2.0 * np.pi / samples) * phase.astype(np.float32)
    half = times.astype(np.float32) + np.float32(0.5)
    taper = np.float32(0.5) - np.float32(0.5) * np.cos(np.float32(2.0 * np.pi / samples) * half)
    table = np.concatenate([taper[:, None] * np.cos(angle), -taper[:, None] * np.sin(angle)], axis=1)
    return jnp.asarray(np.ascontiguousarray(table.T), dtype=jnp.bfloat16)


def pick_rows(channels):
    out = np.zeros((2 * TILE, 2 * channels * TILE), np.float32)
    for part in range(2):
        for a in range(channels):
            start = (part * channels + a) * TILE
            out[part * TILE + a, start : start + TILE] = 1
    return jnp.asarray(out, dtype=jnp.bfloat16)


def spread_bins(channels, bins):
    row = np.arange(channels * TILE)
    col = np.arange(channels * bins)
    same = (row[:, None] // TILE == col[None, :] // bins) & (row[:, None] % TILE == col[None, :] % TILE)
    return jnp.asarray(same.astype(np.float32), dtype=jnp.bfloat16)


def kernel(
    dims, table_in, pick_in, spread_in, records_in, counts_in, gaps_in, result,
    table, pick, spread, records, counts, gaps,
    own, turned, inbox, weights, outgoing, returned,
    load_sem, send_sem, recv_sem, back_send, back_recv,
):
    channels, segments, samples, stations, hours, count = dims
    bins = samples // 2
    span = segments // hours
    groups = bins // TILE
    rows = channels * TILE
    per_station = channels // stations
    me = lax.axis_index("sta")
    kind = lax.rem(me, 4)
    core = lax.rem(kind, 2)
    side = kind // 2

    def at(offset):
        return lax.rem(me + offset + count, count)

    def barrier_signal():
        barrier = pltpu.get_barrier_semaphore()
        for offset in (1, 2, 3, 4, -1, -2, -3, -4):
            pl.semaphore_signal(
                barrier, inc=1, device_id={"sta": at(offset)}, device_id_type=pl.DeviceIdType.MESH
            )

    loads = [
        pltpu.make_async_copy(source, target, load_sem.at[i])
        for i, (source, target) in enumerate(
            (
                (table_in, table), (counts_in, counts), (gaps_in, gaps),
                (pick_in, pick), (spread_in, spread),
            )
        )
    ]
    for load in loads:
        load.start()
    record_loads = [
        pltpu.make_async_copy(records_in.at[c], records.at[c], load_sem.at[len(loads) + c])
        for c in range(channels)
    ]
    for load in record_loads:
        load.start()
    barrier_signal()
    for load in loads:
        load.wait()

    position = lax.broadcasted_iota(jnp.int32, (stations, segments), 1)
    limit = jnp.zeros((stations, segments), jnp.int32)
    for h in range(hours):
        limit = jnp.where(position // span == h, counts[:, h : h + 1], limit)
    valid = jnp.where(lax.rem(position, span) < limit, gaps[...], 0).astype(jnp.float32)
    valid = jnp.concatenate(
        [jnp.broadcast_to(valid[s : s + 1], (per_station, segments)) for s in range(stations)]
        + [jnp.zeros((TILE - channels, segments), jnp.float32)],
        axis=0,
    )
    left = lax.broadcasted_iota(jnp.int32, (TILE, LANES), 1) < span
    for pair in range(hours // 2):
        block = valid[:, pair * LANES : (pair + 1) * LANES]
        first = jnp.where(left, block, 0.0)
        second = jnp.where(left, pltpu.roll(block, span, 1), 0.0)
        own[0, :, 2 * pair * LANES : (2 * pair + 1) * LANES] = first.astype(jnp.bfloat16)
        own[0, :, (2 * pair + 1) * LANES : (2 * pair + 2) * LANES] = second.astype(jnp.bfloat16)

    left_b = lax.broadcasted_iota(jnp.int32, (bins, LANES), 1) < span
    for c in range(channels):
        record_loads[c].wait()
        spectrum = lax.dot_general(table[...], records[c], NT, preferred_element_type=jnp.float32)
        power = jnp.sum(spectrum * spectrum, axis=0, keepdims=True) * (1.0 / samples)
        white = spectrum * (lax.rsqrt(power + EPSILON) * valid[c : c + 1])
        for pair in range(hours // 2):
            re = white[:bins, pair * LANES : (pair + 1) * LANES]
            im = white[bins:, pair * LANES : (pair + 1) * LANES]
            re_r = pltpu.roll(re, span, 1)
            im_r = pltpu.roll(im, span, 1)
            straight = (jnp.where(left_b, re, im_r), jnp.where(left_b, re_r, im))
            across = (jnp.where(left_b, im, -re_r), jnp.where(left_b, im_r, -re))
            for half in range(2):
                lanes = slice((2 * pair + half) * LANES, (2 * pair + half + 1) * LANES)
                flat = straight[half].astype(jnp.bfloat16)
                flat_t = across[half].astype(jnp.bfloat16)
                for g in range(groups):
                    own[1 + g * channels + c, :, lanes] = flat[g * TILE : (g + 1) * TILE]
                    turned[g * channels + c, :, lanes] = flat_t[g * TILE : (g + 1) * TILE]

    pl.semaphore_wait(pltpu.get_barrier_semaphore(), 8)

    part_rows = channels // PARTS

    def where_is(piece):
        if isinstance(piece, int) and piece == 0:
            return pl.ds(0, 1)
        return pl.ds(1 + (piece - 1) * part_rows, part_rows)

    def copy(source, piece, way, slot, target):
        return pltpu.make_async_remote_copy(
            src_ref=source.at[where_is(piece)],
            dst_ref=inbox.at[slot, where_is(piece)],
            send_sem=send_sem.at[way, piece],
            recv_sem=recv_sem.at[slot, piece],
            device_id={"sta": target},
            device_id_type=pl.DeviceIdType.MESH,
        )

    def ahead(piece):
        return copy(own, piece, 0, 1 + 2 * side, at(2 + 2 * side))

    def beside(piece):
        return copy(own, piece, 1, 2 * core, at(1 + 2 * core))

    def relay_twin(piece):
        return copy(inbox.at[1], piece, 2, 2 - 2 * core, at(1 - 2 * core))

    def relay_down(piece):
        return copy(inbox.at[3], piece, 3, 1, at(-2))

    def relay_twin_far(piece):
        return copy(inbox.at[3], piece, 1, 2, at(-1))

    def arrived(slot, piece):
        copy(own, piece, 0, slot, at(1)).wait_recv()

    def send_own(piece):
        ahead(piece).start()

        @pl.when(kind != 3)
        def _():
            beside(piece).start()

    def pass_on(piece):
        @pl.when(side == 1)
        def _():
            arrived(3, piece)
            relay_down(piece).start()

        @pl.when(kind == 3)
        def _():
            relay_twin_far(piece).start()

        arrived(1, piece)
        relay_twin(piece).start()

    send_own(0)
    for piece in range(groups * PARTS):
        send_own(1 + piece)

    def dot_nt(a, b):
        return lax.dot_general(a, b, NT, preferred_element_type=jnp.float32)

    partners = (own,) + tuple(inbox.at[d] for d in range(ROUNDS))
    chunks = (ROUNDS + 1) * rows // COLS
    each = COLS // TILE

    def columns(blocks, n):
        out = []
        for d, block in enumerate(blocks):
            first = max(each * n, d * channels) - d * channels
            last = min(each * (n + 1), (d + 1) * channels) - d * channels
            if first < last:
                out.append(block[first * TILE : last * TILE])
        return jnp.concatenate(out, axis=0) if len(out) > 1 else out[0]

    def widen(ref, h):
        block = ref[0, :, h * LANES : (h + 1) * LANES].astype(jnp.float32)
        return jnp.concatenate(
            [jnp.broadcast_to(block[c : c + 1], (TILE, LANES)) for c in range(channels)], axis=0
        ).astype(jnp.bfloat16)

    def weigh():
        row_id = lax.broadcasted_iota(jnp.int32, (rows, COLS), 0)
        col_id = lax.broadcasted_iota(jnp.int32, (rows, COLS), 1)
        diagonal = lax.rem(row_id, TILE) == lax.rem(col_id, TILE)
        for h in range(hours):
            wide = [widen(ref, h) for ref in partners]
            for n in range(chunks):
                joint = dot_nt(wide[0], columns(wide, n))
                weights[h, n] = jnp.where(diagonal, 1.0 / (hours * jnp.maximum(joint, 1.0)), 0.0)

    def correlate(g):
        at_rows = pl.ds(1 + g * channels, channels)
        t_rows = pl.ds(g * channels, channels)
        picked = []
        for n in range(chunks):
            re = jnp.zeros((rows, COLS), jnp.float32)
            im = jnp.zeros((rows, COLS), jnp.float32)
            for h in range(hours):
                lanes = slice(h * LANES, (h + 1) * LANES)
                blocks = [ref[at_rows, :, lanes].reshape(rows, LANES) for ref in partners]
                mine_t = turned[t_rows, :, lanes].reshape(rows, LANES)
                product = dot_nt(jnp.concatenate([blocks[0], mine_t], axis=0), columns(blocks, n))
                scale = weights[h, n]
                re = re + product[:rows] * scale
                im = im + product[rows:] * scale
            both = jnp.concatenate([re, im], axis=0).astype(jnp.bfloat16)
            picked.append(jnp.dot(pick[...], both, preferred_element_type=jnp.float32))
        return jnp.concatenate(picked, axis=1)

    tall = 2 * TILE

    def give_back(d, g):
        return pltpu.make_async_remote_copy(
            src_ref=outgoing.at[g, pl.ds(d * tall, tall)],
            dst_ref=returned.at[g, pl.ds((d - 1) * tall, tall)],
            send_sem=back_send.at[d - 1, g],
            recv_sem=back_recv.at[d - 1, g],
            device_id={"sta": at(-d)},
            device_id_type=pl.DeviceIdType.MESH,
        )

    def finish(ref, slots):
        height = len(slots) * tall
        group_of = lax.rem(lax.broadcasted_iota(jnp.int32, (height, COLS), 1), bins) // TILE
        flat = ref[...].reshape(groups * height, rows)
        for n in range(channels * bins // COLS):
            wide = jnp.dot(
                flat, spread[:, n * COLS : (n + 1) * COLS], preferred_element_type=jnp.float32
            )
            merged = wide[:height]
            for g in range(1, groups):
                merged = jnp.where(group_of == g, wide[g * height : (g + 1) * height], merged)
            for i, (slot, flip) in enumerate(slots):
                for part in range(2):
                    for k in range(COLS // bins):
                        start = i * tall + part * TILE
                        value = merged[start : start + TILE, k * bins : (k + 1) * bins]
                        if flip and part == 1:
                            value = -value
                        result[slot, part, n * (COLS // bins) + k] = value.astype(jnp.bfloat16)

    pass_on(0)
    arrived(0, 0)
    arrived(2, 0)
    weigh()

    @pl.loop(0, groups)
    def _(g):
        pieces = [1 + g * PARTS + part for part in range(PARTS)]
        for piece in pieces:
            pass_on(piece)
        for piece in pieces:
            arrived(0, piece)
            arrived(2, piece)
        picked = correlate(g)
        for d in range(1, ROUNDS + 1):
            outgoing[g, d * tall : (d + 1) * tall] = picked[:, d * rows : (d + 1) * rows].astype(
                jnp.bfloat16
            )
            give_back(d, g).start()
        outgoing[g, :tall] = picked[:, :rows].astype(jnp.bfloat16)

    finish(outgoing, [(ROUNDS - d, False) for d in range(ROUNDS + 1)])

    @pl.loop(0, groups)
    def _(g):
        for d in range(1, ROUNDS + 1):
            give_back(d, g).wait_recv()

    finish(returned, [(ROUNDS + d, True) for d in range(1, ROUNDS + 1)])

    @pl.loop(0, groups)
    def _(g):
        for d in range(1, ROUNDS + 1):
            give_back(d, g).wait_send()

    def sent(piece):
        ahead(piece).wait_send()
        beside(piece).wait_send()
        relay_twin(piece).wait_send()

        @pl.when(side == 1)
        def _():
            relay_down(piece).wait_send()

    sent(0)

    @pl.loop(0, groups * PARTS)
    def _(i):
        sent(i + 1)


def per_device(count, records, counts, gap_mask):
    channels, segments, samples = records.shape
    stations, hours = counts.shape
    bins = samples // 2
    groups = bins // TILE
    rows = channels * TILE
    blocks = 1 + groups * channels
    wide = hours * LANES
    dims = (channels, segments, samples, stations, hours, count)
    pieces = groups * PARTS + 1
    result = pl.pallas_call(
        functools.partial(kernel, dims),
        out_shape=jax.ShapeDtypeStruct((2 * ROUNDS + 1, 2, channels, TILE, bins), jnp.bfloat16),
        in_specs=[pl.BlockSpec(memory_space=pltpu.HBM)] * 6,
        out_specs=pl.BlockSpec(memory_space=pltpu.VMEM),
        scratch_shapes=[
            pltpu.VMEM((samples, samples), jnp.bfloat16),
            pltpu.VMEM((2 * TILE, 2 * rows), jnp.bfloat16),
            pltpu.VMEM((rows, channels * bins), jnp.bfloat16),
            pltpu.VMEM((channels, segments, samples), jnp.bfloat16),
            pltpu.VMEM((stations, hours), jnp.int32),
            pltpu.VMEM((stations, segments), jnp.int32),
            pltpu.VMEM((blocks, TILE, wide), jnp.bfloat16),
            pltpu.VMEM((blocks - 1, TILE, wide), jnp.bfloat16),
            pltpu.VMEM((ROUNDS + 1, blocks, TILE, wide), jnp.bfloat16),
            pltpu.VMEM((hours, (ROUNDS + 1) * rows // COLS, rows, COLS), jnp.float32),
            pltpu.VMEM((groups, (ROUNDS + 1) * 2 * TILE, rows), jnp.bfloat16),
            pltpu.VMEM((groups, ROUNDS * 2 * TILE, rows), jnp.bfloat16),
            pltpu.SemaphoreType.DMA((5 + channels,)),
            pltpu.SemaphoreType.DMA((4, pieces)),
            pltpu.SemaphoreType.DMA((4, pieces)),
            pltpu.SemaphoreType.DMA((ROUNDS, groups)),
            pltpu.SemaphoreType.DMA((ROUNDS, groups)),
        ],
        compiler_params=pltpu.CompilerParams(
            collective_id=0, has_side_effects=True, vmem_limit_bytes=54 * 1024 * 1024
        ),
    )(
        fourier_rows(samples), pick_rows(channels), spread_bins(channels, bins),
        records, counts, gap_mask,
    )
    result = result[:, :, :, :channels]
    below = jnp.transpose(result[: ROUNDS + 1], (0, 1, 3, 2, 4))
    return jnp.concatenate([below, result[ROUNDS + 1 :]], axis=0)


def solution(mesh):
    count = mesh.shape["sta"]
    return jax.shard_map(
        functools.partial(per_device, count),
        mesh=mesh,
        in_specs=(P(("days", "sta"), None, None), P(("days", "sta"), None), P(("days", "sta"), None)),
        out_specs=P(None, None, ("days", "sta"), None, None),
        check_vma=False,
    )
```

```python
import functools

import jax
import jax.numpy as jnp
import numpy as np
from jax import lax
from jax.experimental import pallas as pl
from jax.experimental.pallas import tpu as pltpu
from jax.sharding import PartitionSpec as P

ROUNDS = 3
TILE = 16
LANES = 128
PARTS = 2
COLS = 256
EPSILON = 1e-06
NT = (((1,), (1,)), ((), ()))


def fourier_rows(samples):
    bins = samples // 2
    times = np.arange(samples, dtype=np.int32)
    phase = (times[:, None] * np.arange(bins, dtype=np.int32)[None, :]) % samples
    angle = np.float32(2.0 * np.pi / samples) * phase.astype(np.float32)
    half = times.astype(np.float32) + np.float32(0.5)
    taper = np.float32(0.5) - np.float32(0.5) * np.cos(np.float32(2.0 * np.pi / samples) * half)
    table = np.concatenate([taper[:, None] * np.cos(angle), -taper[:, None] * np.sin(angle)], axis=1)
    return jnp.asarray(np.ascontiguousarray(table.T), dtype=jnp.bfloat16)


def pick_rows(channels):
    out = np.zeros((2 * TILE, 2 * channels * TILE), np.float32)
    for part in range(2):
        for a in range(channels):
            start = (part * channels + a) * TILE
            out[part * TILE + a, start : start + TILE] = 1
    return jnp.asarray(out, dtype=jnp.bfloat16)


def spread_bins(channels, bins):
    row = np.arange(channels * TILE)
    col = np.arange(channels * bins)
    same = (row[:, None] // TILE == col[None, :] // bins) & (row[:, None] % TILE == col[None, :] % TILE)
    return jnp.asarray(same.astype(np.float32), dtype=jnp.bfloat16)


def kernel(
    dims, table_in, pick_in, spread_in, records_in, counts_in, gaps_in, result,
    table, pick, spread, records, counts, gaps,
    own, turned, inbox, weights, outgoing, returned,
    load_sem, send_sem, recv_sem, back_send, back_recv,
):
    channels, segments, samples, stations, hours, count = dims
    bins = samples // 2
    span = segments // hours
    groups = bins // TILE
    rows = channels * TILE
    per_station = channels // stations
    me = lax.axis_index("sta")
    kind = lax.rem(me, 4)
    core = lax.rem(kind, 2)
    far = kind // 3

    def at(offset):
        return lax.rem(me + offset + count, count)

    def barrier_signal():
        barrier = pltpu.get_barrier_semaphore()
        for offset in (1, 2, 3, 4, -1, -2, -3, -4):
            pl.semaphore_signal(
                barrier, inc=1, device_id={"sta": at(offset)}, device_id_type=pl.DeviceIdType.MESH
            )

    loads = [
        pltpu.make_async_copy(source, target, load_sem.at[i])
        for i, (source, target) in enumerate(
            (
                (table_in, table), (counts_in, counts), (gaps_in, gaps),
                (pick_in, pick), (spread_in, spread),
            )
        )
    ]
    for load in loads:
        load.start()
    record_loads = [
        pltpu.make_async_copy(records_in.at[c], records.at[c], load_sem.at[len(loads) + c])
        for c in range(channels)
    ]
    for load in record_loads:
        load.start()
    barrier_signal()
    for load in loads:
        load.wait()

    position = lax.broadcasted_iota(jnp.int32, (stations, segments), 1)
    limit = jnp.zeros((stations, segments), jnp.int32)
    for h in range(hours):
        limit = jnp.where(position // span == h, counts[:, h : h + 1], limit)
    valid = jnp.where(lax.rem(position, span) < limit, gaps[...], 0).astype(jnp.float32)
    valid = jnp.concatenate(
        [jnp.broadcast_to(valid[s : s + 1], (per_station, segments)) for s in range(stations)]
        + [jnp.zeros((TILE - channels, segments), jnp.float32)],
        axis=0,
    )
    left = lax.broadcasted_iota(jnp.int32, (TILE, LANES), 1) < span
    for pair in range(hours // 2):
        block = valid[:, pair * LANES : (pair + 1) * LANES]
        first = jnp.where(left, block, 0.0)
        second = jnp.where(left, pltpu.roll(block, span, 1), 0.0)
        own[0, :, 2 * pair * LANES : (2 * pair + 1) * LANES] = first.astype(jnp.bfloat16)
        own[0, :, (2 * pair + 1) * LANES : (2 * pair + 2) * LANES] = second.astype(jnp.bfloat16)

    left_b = lax.broadcasted_iota(jnp.int32, (bins, LANES), 1) < span
    for c in range(channels):
        record_loads[c].wait()
        spectrum = lax.dot_general(table[...], records[c], NT, preferred_element_type=jnp.float32)
        power = jnp.sum(spectrum * spectrum, axis=0, keepdims=True) * (1.0 / samples)
        white = spectrum * (lax.rsqrt(power + EPSILON) * valid[c : c + 1])
        for pair in range(hours // 2):
            re = white[:bins, pair * LANES : (pair + 1) * LANES]
            im = white[bins:, pair * LANES : (pair + 1) * LANES]
            re_r = pltpu.roll(re, span, 1)
            im_r = pltpu.roll(im, span, 1)
            straight = (jnp.where(left_b, re, im_r), jnp.where(left_b, re_r, im))
            across = (jnp.where(left_b, im, -re_r), jnp.where(left_b, im_r, -re))
            for half in range(2):
                lanes = slice((2 * pair + half) * LANES, (2 * pair + half + 1) * LANES)
                flat = straight[half].astype(jnp.bfloat16)
                flat_t = across[half].astype(jnp.bfloat16)
                for g in range(groups):
                    own[1 + g * channels + c, :, lanes] = flat[g * TILE : (g + 1) * TILE]
                    turned[g * channels + c, :, lanes] = flat_t[g * TILE : (g + 1) * TILE]

    pl.semaphore_wait(pltpu.get_barrier_semaphore(), 8)

    part_rows = channels // PARTS

    def where_is(piece):
        if isinstance(piece, int) and piece == 0:
            return pl.ds(0, 1)
        return pl.ds(1 + (piece - 1) * part_rows, part_rows)

    def copy(source, piece, way, slot, target):
        return pltpu.make_async_remote_copy(
            src_ref=source.at[where_is(piece)],
            dst_ref=inbox.at[slot, where_is(piece)],
            send_sem=send_sem.at[way, piece],
            recv_sem=recv_sem.at[slot, piece],
            device_id={"sta": target},
            device_id_type=pl.DeviceIdType.MESH,
        )

    def ahead(piece):
        return copy(own, piece, 0, 1 + 2 * far, at(2 + 2 * far))

    def beside(piece):
        return copy(own, piece, 1, 2 * core, at(1 + 2 * core))

    def relay_twin(piece):
        return copy(inbox.at[1], piece, 2, 2 - 2 * core, at(1 - 2 * core))

    def relay_down(piece):
        return copy(inbox.at[3], piece, 3, 1, at(-2))

    def relay_twin_far(piece):
        return copy(inbox.at[3], piece, 1, 2, at(-1))

    def arrived(slot, piece):
        copy(own, piece, 0, slot, at(1)).wait_recv()

    def send_own(piece):
        ahead(piece).start()

        @pl.when(far == 0)
        def _():
            beside(piece).start()

    def pass_on(piece):
        @pl.when(far == 1)
        def _():
            arrived(3, piece)
            relay_down(piece).start()
            relay_twin_far(piece).start()

        arrived(1, piece)
        relay_twin(piece).start()

    send_own(0)
    for piece in range(groups * PARTS):
        send_own(1 + piece)

    def dot_nt(a, b):
        return lax.dot_general(a, b, NT, preferred_element_type=jnp.float32)

    partners = (own,) + tuple(inbox.at[d] for d in range(ROUNDS))
    chunks = (ROUNDS + 1) * rows // COLS
    each = COLS // TILE

    def columns(blocks, n):
        out = []
        for d, block in enumerate(blocks):
            first = max(each * n, d * channels) - d * channels
            last = min(each * (n + 1), (d + 1) * channels) - d * channels
            if first < last:
                out.append(block[first * TILE : last * TILE])
        return jnp.concatenate(out, axis=0) if len(out) > 1 else out[0]

    def widen(ref, h):
        block = ref[0, :, h * LANES : (h + 1) * LANES].astype(jnp.float32)
        return jnp.concatenate(
            [jnp.broadcast_to(block[c : c + 1], (TILE, LANES)) for c in range(channels)], axis=0
        ).astype(jnp.bfloat16)

    def weigh():
        row_id = lax.broadcasted_iota(jnp.int32, (rows, COLS), 0)
        col_id = lax.broadcasted_iota(jnp.int32, (rows, COLS), 1)
        diagonal = lax.rem(row_id, TILE) == lax.rem(col_id, TILE)
        for h in range(hours):
            wide = [widen(ref, h) for ref in partners]
            for n in range(chunks):
                joint = dot_nt(wide[0], columns(wide, n))
                weights[h, n] = jnp.where(diagonal, 1.0 / (hours * jnp.maximum(joint, 1.0)), 0.0)

    def correlate(g):
        at_rows = pl.ds(1 + g * channels, channels)
        t_rows = pl.ds(g * channels, channels)
        picked = []
        for n in range(chunks):
            re = jnp.zeros((rows, COLS), jnp.float32)
            im = jnp.zeros((rows, COLS), jnp.float32)
            for h in range(hours):
                lanes = slice(h * LANES, (h + 1) * LANES)
                blocks = [ref[at_rows, :, lanes].reshape(rows, LANES) for ref in partners]
                mine_t = turned[t_rows, :, lanes].reshape(rows, LANES)
                product = dot_nt(jnp.concatenate([blocks[0], mine_t], axis=0), columns(blocks, n))
                scale = weights[h, n]
                re = re + product[:rows] * scale
                im = im + product[rows:] * scale
            both = jnp.concatenate([re, im], axis=0).astype(jnp.bfloat16)
            picked.append(jnp.dot(pick[...], both, preferred_element_type=jnp.float32))
        return jnp.concatenate(picked, axis=1)

    tall = 2 * TILE

    def give_back(d, g):
        return pltpu.make_async_remote_copy(
            src_ref=outgoing.at[g, pl.ds(d * tall, tall)],
            dst_ref=returned.at[g, pl.ds((d - 1) * tall, tall)],
            send_sem=back_send.at[d - 1, g],
            recv_sem=back_recv.at[d - 1, g],
            device_id={"sta": at(-d)},
            device_id_type=pl.DeviceIdType.MESH,
        )

    def finish(ref, slots):
        height = len(slots) * tall
        group_of = lax.rem(lax.broadcasted_iota(jnp.int32, (height, COLS), 1), bins) // TILE
        flat = ref[...].reshape(groups * height, rows)
        for n in range(channels * bins // COLS):
            wide = jnp.dot(
                flat, spread[:, n * COLS : (n + 1) * COLS], preferred_element_type=jnp.float32
            )
            merged = wide[:height]
            for g in range(1, groups):
                merged = jnp.where(group_of == g, wide[g * height : (g + 1) * height], merged)
            for i, (slot, flip) in enumerate(slots):
                for part in range(2):
                    for k in range(COLS // bins):
                        start = i * tall + part * TILE
                        value = merged[start : start + TILE, k * bins : (k + 1) * bins]
                        if flip and part == 1:
                            value = -value
                        result[slot, part, n * (COLS // bins) + k] = value.astype(jnp.bfloat16)

    pass_on(0)
    arrived(0, 0)
    arrived(2, 0)
    weigh()

    @pl.loop(0, groups)
    def _(g):
        pieces = [1 + g * PARTS + part for part in range(PARTS)]
        for piece in pieces:
            pass_on(piece)
        for piece in pieces:
            arrived(0, piece)
            arrived(2, piece)
        picked = correlate(g)
        for d in range(1, ROUNDS + 1):
            outgoing[g, d * tall : (d + 1) * tall] = picked[:, d * rows : (d + 1) * rows].astype(
                jnp.bfloat16
            )
            give_back(d, g).start()
        outgoing[g, :tall] = picked[:, :rows].astype(jnp.bfloat16)

    finish(outgoing, [(ROUNDS - d, False) for d in range(ROUNDS + 1)])

    @pl.loop(0, groups)
    def _(g):
        for d in range(1, ROUNDS + 1):
            give_back(d, g).wait_recv()

    finish(returned, [(ROUNDS + d, True) for d in range(1, ROUNDS + 1)])

    @pl.loop(0, groups)
    def _(g):
        for d in range(1, ROUNDS + 1):
            give_back(d, g).wait_send()

    def sent(piece):
        ahead(piece).wait_send()
        beside(piece).wait_send()
        relay_twin(piece).wait_send()

        @pl.when(far == 1)
        def _():
            relay_down(piece).wait_send()

    sent(0)

    @pl.loop(0, groups * PARTS)
    def _(i):
        sent(i + 1)


def per_device(count, records, counts, gap_mask):
    channels, segments, samples = records.shape
    stations, hours = counts.shape
    bins = samples // 2
    groups = bins // TILE
    rows = channels * TILE
    blocks = 1 + groups * channels
    wide = hours * LANES
    dims = (channels, segments, samples, stations, hours, count)
    pieces = groups * PARTS + 1
    result = pl.pallas_call(
        functools.partial(kernel, dims),
        out_shape=jax.ShapeDtypeStruct((2 * ROUNDS + 1, 2, channels, TILE, bins), jnp.bfloat16),
        in_specs=[pl.BlockSpec(memory_space=pltpu.HBM)] * 6,
        out_specs=pl.BlockSpec(memory_space=pltpu.VMEM),
        scratch_shapes=[
            pltpu.VMEM((samples, samples), jnp.bfloat16),
            pltpu.VMEM((2 * TILE, 2 * rows), jnp.bfloat16),
            pltpu.VMEM((rows, channels * bins), jnp.bfloat16),
            pltpu.VMEM((channels, segments, samples), jnp.bfloat16),
            pltpu.VMEM((stations, hours), jnp.int32),
            pltpu.VMEM((stations, segments), jnp.int32),
            pltpu.VMEM((blocks, TILE, wide), jnp.bfloat16),
            pltpu.VMEM((blocks - 1, TILE, wide), jnp.bfloat16),
            pltpu.VMEM((ROUNDS + 1, blocks, TILE, wide), jnp.bfloat16),
            pltpu.VMEM((hours, (ROUNDS + 1) * rows // COLS, rows, COLS), jnp.float32),
            pltpu.VMEM((groups, (ROUNDS + 1) * 2 * TILE, rows), jnp.bfloat16),
            pltpu.VMEM((groups, ROUNDS * 2 * TILE, rows), jnp.bfloat16),
            pltpu.SemaphoreType.DMA((5 + channels,)),
            pltpu.SemaphoreType.DMA((4, pieces)),
            pltpu.SemaphoreType.DMA((4, pieces)),
            pltpu.SemaphoreType.DMA((ROUNDS, groups)),
            pltpu.SemaphoreType.DMA((ROUNDS, groups)),
        ],
        compiler_params=pltpu.CompilerParams(
            collective_id=0, has_side_effects=True, vmem_limit_bytes=54 * 1024 * 1024
        ),
    )(
        fourier_rows(samples), pick_rows(channels), spread_bins(channels, bins),
        records, counts, gap_mask,
    )
    result = result[:, :, :, :channels]
    below = jnp.transpose(result[: ROUNDS + 1], (0, 1, 3, 2, 4))
    return jnp.concatenate([below, result[ROUNDS + 1 :]], axis=0)


def solution(mesh):
    count = mesh.shape["sta"]
    return jax.shard_map(
        functools.partial(per_device, count),
        mesh=mesh,
        in_specs=(P(("days", "sta"), None, None), P(("days", "sta"), None), P(("days", "sta"), None)),
        out_specs=P(None, None, ("days", "sta"), None, None),
        check_vma=False,
    )
```

```python
import functools

import jax
import jax.numpy as jnp
import numpy as np
from jax import lax
from jax.experimental import pallas as pl
from jax.experimental.pallas import tpu as pltpu
from jax.sharding import PartitionSpec as P

ROUNDS = 3
TILE = 16
LANES = 128
PARTS = 2
COLS = 256
EARLY = 2
TURN = 4
EPSILON = 1e-06
NT = (((1,), (1,)), ((), ()))


def fourier_rows(samples):
    bins = samples // 2
    times = np.arange(samples, dtype=np.int32)
    phase = (times[:, None] * np.arange(bins, dtype=np.int32)[None, :]) % samples
    angle = np.float32(2.0 * np.pi / samples) * phase.astype(np.float32)
    half = times.astype(np.float32) + np.float32(0.5)
    taper = np.float32(0.5) - np.float32(0.5) * np.cos(np.float32(2.0 * np.pi / samples) * half)
    table = np.concatenate([taper[:, None] * np.cos(angle), -taper[:, None] * np.sin(angle)], axis=1)
    return jnp.asarray(np.ascontiguousarray(table.T), dtype=jnp.bfloat16)


def pick_rows(channels):
    out = np.zeros((2 * TILE, 2 * channels * TILE), np.float32)
    for part in range(2):
        for a in range(channels):
            start = (part * channels + a) * TILE
            out[part * TILE + a, start : start + TILE] = 1
    return jnp.asarray(out, dtype=jnp.bfloat16)


def spread_bins(channels, bins):
    row = np.arange(channels * TILE)
    col = np.arange(channels * bins)
    same = (row[:, None] // TILE == col[None, :] // bins) & (row[:, None] % TILE == col[None, :] % TILE)
    return jnp.asarray(same.astype(np.float32), dtype=jnp.bfloat16)


def kernel(
    dims, table_in, pick_in, spread_in, records_in, counts_in, gaps_in, result,
    table, pick, spread, records, counts, gaps,
    own, turned, inbox, weights, outgoing, returned,
    load_sem, send_sem, recv_sem, back_send, back_recv,
):
    channels, segments, samples, stations, hours, count = dims
    bins = samples // 2
    span = segments // hours
    groups = bins // TILE
    rows = channels * TILE
    per_station = channels // stations
    me = lax.axis_index("sta")
    kind = lax.rem(me, 4)
    core = lax.rem(kind, 2)
    far = kind // 3

    def at(offset):
        return lax.rem(me + offset + count, count)

    def barrier_signal():
        barrier = pltpu.get_barrier_semaphore()
        for offset in (1, 2, 3, 4, -1, -2, -3, -4):
            pl.semaphore_signal(
                barrier, inc=1, device_id={"sta": at(offset)}, device_id_type=pl.DeviceIdType.MESH
            )

    loads = [
        pltpu.make_async_copy(source, target, load_sem.at[i])
        for i, (source, target) in enumerate(
            (
                (table_in, table), (counts_in, counts), (gaps_in, gaps),
                (pick_in, pick), (spread_in, spread),
            )
        )
    ]
    for load in loads:
        load.start()
    record_loads = [
        pltpu.make_async_copy(records_in.at[c], records.at[c], load_sem.at[len(loads) + c])
        for c in range(channels)
    ]
    for load in record_loads:
        load.start()
    barrier_signal()
    part_rows = channels // PARTS
    for load in loads:
        load.wait()

    position = lax.broadcasted_iota(jnp.int32, (stations, segments), 1)
    limit = jnp.zeros((stations, segments), jnp.int32)
    for h in range(hours):
        limit = jnp.where(position // span == h, counts[:, h : h + 1], limit)
    valid = jnp.where(lax.rem(position, span) < limit, gaps[...], 0).astype(jnp.float32)
    valid = jnp.concatenate(
        [jnp.broadcast_to(valid[s : s + 1], (per_station, segments)) for s in range(stations)]
        + [jnp.zeros((TILE - channels, segments), jnp.float32)],
        axis=0,
    )
    left = lax.broadcasted_iota(jnp.int32, (TILE, LANES), 1) < span
    for pair in range(hours // 2):
        block = valid[:, pair * LANES : (pair + 1) * LANES]
        first = jnp.where(left, block, 0.0)
        second = jnp.where(left, pltpu.roll(block, span, 1), 0.0)
        own[0, :, 2 * pair * LANES : (2 * pair + 1) * LANES] = first.astype(jnp.bfloat16)
        own[0, :, (2 * pair + 1) * LANES : (2 * pair + 2) * LANES] = second.astype(jnp.bfloat16)

    def where_is(piece):
        if isinstance(piece, int) and piece == 0:
            return pl.ds(0, 1)
        return pl.ds(1 + (piece - 1) * part_rows, part_rows)

    def copy(source, piece, way, slot, target):
        return pltpu.make_async_remote_copy(
            src_ref=source.at[where_is(piece)],
            dst_ref=inbox.at[slot, where_is(piece)],
            send_sem=send_sem.at[way, piece],
            recv_sem=recv_sem.at[slot, piece],
            device_id={"sta": target},
            device_id_type=pl.DeviceIdType.MESH,
        )

    def ahead(piece):
        return copy(own, piece, 0, 1 + 2 * far, at(2 + 2 * far))

    def beside(piece):
        return copy(own, piece, 1, 2 * core, at(1 + 2 * core))

    def relay_twin(piece):
        return copy(inbox.at[1], piece, 2, 2 - 2 * core, at(1 - 2 * core))

    def relay_down(piece):
        return copy(inbox.at[3], piece, 3, 1, at(-2))

    def relay_twin_far(piece):
        return copy(inbox.at[3], piece, 1, 2, at(-1))

    def arrived(slot, piece):
        copy(own, piece, 0, slot, at(1)).wait_recv()

    def send_own(piece):
        ahead(piece).start()

        @pl.when(far == 0)
        def _():
            beside(piece).start()

    def pass_on(piece):
        @pl.when(far == 1)
        def _():
            arrived(3, piece)
            relay_down(piece).start()
            relay_twin_far(piece).start()

        arrived(1, piece)
        relay_twin(piece).start()

    left_b = lax.broadcasted_iota(jnp.int32, (bins, LANES), 1) < span

    def whiten(c):
        record_loads[c].wait()
        spectrum = lax.dot_general(table[...], records[c], NT, preferred_element_type=jnp.float32)
        power = jnp.sum(spectrum * spectrum, axis=0, keepdims=True) * (1.0 / samples)
        white = spectrum * (lax.rsqrt(power + EPSILON) * valid[c : c + 1])
        for pair in range(hours // 2):
            re = white[:bins, pair * LANES : (pair + 1) * LANES]
            im = white[bins:, pair * LANES : (pair + 1) * LANES]
            straight = (
                jnp.where(left_b, re, pltpu.roll(im, span, 1)),
                jnp.where(left_b, pltpu.roll(re, span, 1), im),
            )
            for half in range(2):
                lanes = slice((2 * pair + half) * LANES, (2 * pair + half + 1) * LANES)
                flat = straight[half].astype(jnp.bfloat16)
                for g in range(groups):
                    own[1 + g * channels + c, :, lanes] = flat[g * TILE : (g + 1) * TILE]

    early = min(EARLY, groups)
    for part in range(PARTS):
        for c in range(part * part_rows, (part + 1) * part_rows):
            whiten(c)
        if part == 0:
            pl.semaphore_wait(pltpu.get_barrier_semaphore(), 8)
            send_own(0)
        for g in range(early):
            send_own(1 + g * PARTS + part)
    for piece in range(early * PARTS, groups * PARTS):
        send_own(1 + piece)

    sign = jnp.where(left, 1.0, -1.0)

    @pl.loop(0, groups * channels // TURN)
    def _(i):
        for r in range(TURN):
            for h in range(hours):
                lanes = slice(h * LANES, (h + 1) * LANES)
                block = own[1 + i * TURN + r, :, lanes].astype(jnp.float32)
                turned[i * TURN + r, :, lanes] = (pltpu.roll(block, span, 1) * sign).astype(jnp.bfloat16)

    def dot_nt(a, b):
        return lax.dot_general(a, b, NT, preferred_element_type=jnp.float32)

    partners = (own,) + tuple(inbox.at[d] for d in range(ROUNDS))
    chunks = (ROUNDS + 1) * rows // COLS
    each = COLS // TILE

    def columns(blocks, n):
        out = []
        for d, block in enumerate(blocks):
            first = max(each * n, d * channels) - d * channels
            last = min(each * (n + 1), (d + 1) * channels) - d * channels
            if first < last:
                out.append(block[first * TILE : last * TILE])
        return jnp.concatenate(out, axis=0) if len(out) > 1 else out[0]

    def widen(ref, h):
        block = ref[0, :, h * LANES : (h + 1) * LANES].astype(jnp.float32)
        return jnp.concatenate(
            [jnp.broadcast_to(block[c : c + 1], (TILE, LANES)) for c in range(channels)], axis=0
        ).astype(jnp.bfloat16)

    def weigh():
        row_id = lax.broadcasted_iota(jnp.int32, (rows, COLS), 0)
        col_id = lax.broadcasted_iota(jnp.int32, (rows, COLS), 1)
        diagonal = lax.rem(row_id, TILE) == lax.rem(col_id, TILE)
        for h in range(hours):
            wide = [widen(ref, h) for ref in partners]
            for n in range(chunks):
                joint = dot_nt(wide[0], columns(wide, n))
                weights[h, n] = jnp.where(diagonal, 1.0 / (hours * jnp.maximum(joint, 1.0)), 0.0)

    def correlate(g):
        at_rows = pl.ds(1 + g * channels, channels)
        t_rows = pl.ds(g * channels, channels)
        picked = []
        for n in range(chunks):
            re = jnp.zeros((rows, COLS), jnp.float32)
            im = jnp.zeros((rows, COLS), jnp.float32)
            for h in range(hours):
                lanes = slice(h * LANES, (h + 1) * LANES)
                blocks = [ref[at_rows, :, lanes].reshape(rows, LANES) for ref in partners]
                mine_t = turned[t_rows, :, lanes].reshape(rows, LANES)
                product = dot_nt(jnp.concatenate([blocks[0], mine_t], axis=0), columns(blocks, n))
                scale = weights[h, n]
                re = re + product[:rows] * scale
                im = im + product[rows:] * scale
            both = jnp.concatenate([re, im], axis=0).astype(jnp.bfloat16)
            picked.append(jnp.dot(pick[...], both, preferred_element_type=jnp.float32))
        return jnp.concatenate(picked, axis=1)

    tall = 2 * TILE

    def give_back(d, g):
        return pltpu.make_async_remote_copy(
            src_ref=outgoing.at[g, pl.ds(d * tall, tall)],
            dst_ref=returned.at[g, pl.ds((d - 1) * tall, tall)],
            send_sem=back_send.at[d - 1, g],
            recv_sem=back_recv.at[d - 1, g],
            device_id={"sta": at(-d)},
            device_id_type=pl.DeviceIdType.MESH,
        )

    def finish(ref, slots):
        height = len(slots) * tall
        group_of = lax.rem(lax.broadcasted_iota(jnp.int32, (height, COLS), 1), bins) // TILE
        flat = ref[...].reshape(groups * height, rows)
        for n in range(channels * bins // COLS):
            wide = jnp.dot(
                flat, spread[:, n * COLS : (n + 1) * COLS], preferred_element_type=jnp.float32
            )
            merged = wide[:height]
            for g in range(1, groups):
                merged = jnp.where(group_of == g, wide[g * height : (g + 1) * height], merged)
            for i, (slot, flip) in enumerate(slots):
                for part in range(2):
                    for k in range(COLS // bins):
                        start = i * tall + part * TILE
                        value = merged[start : start + TILE, k * bins : (k + 1) * bins]
                        if flip and part == 1:
                            value = -value
                        result[slot, part, n * (COLS // bins) + k] = value.astype(jnp.bfloat16)

    pass_on(0)
    arrived(0, 0)
    arrived(2, 0)
    weigh()

    @pl.loop(0, groups)
    def _(g):
        pieces = [1 + g * PARTS + part for part in range(PARTS)]
        for piece in pieces:
            pass_on(piece)
        for piece in pieces:
            arrived(0, piece)
            arrived(2, piece)
        picked = correlate(g)
        for d in range(1, ROUNDS + 1):
            outgoing[g, d * tall : (d + 1) * tall] = picked[:, d * rows : (d + 1) * rows].astype(
                jnp.bfloat16
            )
            give_back(d, g).start()
        outgoing[g, :tall] = picked[:, :rows].astype(jnp.bfloat16)

    finish(outgoing, [(ROUNDS - d, False) for d in range(ROUNDS + 1)])

    @pl.loop(0, groups)
    def _(g):
        for d in range(1, ROUNDS + 1):
            give_back(d, g).wait_recv()

    finish(returned, [(ROUNDS + d, True) for d in range(1, ROUNDS + 1)])

    @pl.loop(0, groups)
    def _(g):
        for d in range(1, ROUNDS + 1):
            give_back(d, g).wait_send()

    def sent(piece):
        ahead(piece).wait_send()
        beside(piece).wait_send()
        relay_twin(piece).wait_send()

        @pl.when(far == 1)
        def _():
            relay_down(piece).wait_send()

    sent(0)

    @pl.loop(0, groups * PARTS)
    def _(i):
        sent(i + 1)


def per_device(count, records, counts, gap_mask):
    channels, segments, samples = records.shape
    stations, hours = counts.shape
    bins = samples // 2
    groups = bins // TILE
    rows = channels * TILE
    blocks = 1 + groups * channels
    wide = hours * LANES
    dims = (channels, segments, samples, stations, hours, count)
    pieces = groups * PARTS + 1
    result = pl.pallas_call(
        functools.partial(kernel, dims),
        out_shape=jax.ShapeDtypeStruct((2 * ROUNDS + 1, 2, channels, TILE, bins), jnp.bfloat16),
        in_specs=[pl.BlockSpec(memory_space=pltpu.HBM)] * 6,
        out_specs=pl.BlockSpec(memory_space=pltpu.VMEM),
        scratch_shapes=[
            pltpu.VMEM((samples, samples), jnp.bfloat16),
            pltpu.VMEM((2 * TILE, 2 * rows), jnp.bfloat16),
            pltpu.VMEM((rows, channels * bins), jnp.bfloat16),
            pltpu.VMEM((channels, segments, samples), jnp.bfloat16),
            pltpu.VMEM((stations, hours), jnp.int32),
            pltpu.VMEM((stations, segments), jnp.int32),
            pltpu.VMEM((blocks, TILE, wide), jnp.bfloat16),
            pltpu.VMEM((blocks - 1, TILE, wide), jnp.bfloat16),
            pltpu.VMEM((ROUNDS + 1, blocks, TILE, wide), jnp.bfloat16),
            pltpu.VMEM((hours, (ROUNDS + 1) * rows // COLS, rows, COLS), jnp.float32),
            pltpu.VMEM((groups, (ROUNDS + 1) * 2 * TILE, rows), jnp.bfloat16),
            pltpu.VMEM((groups, ROUNDS * 2 * TILE, rows), jnp.bfloat16),
            pltpu.SemaphoreType.DMA((5 + channels,)),
            pltpu.SemaphoreType.DMA((4, pieces)),
            pltpu.SemaphoreType.DMA((4, pieces)),
            pltpu.SemaphoreType.DMA((ROUNDS, groups)),
            pltpu.SemaphoreType.DMA((ROUNDS, groups)),
        ],
        compiler_params=pltpu.CompilerParams(
            collective_id=0, has_side_effects=True, vmem_limit_bytes=54 * 1024 * 1024
        ),
    )(
        fourier_rows(samples), pick_rows(channels), spread_bins(channels, bins),
        records, counts, gap_mask,
    )
    result = result[:, :, :, :channels]
    below = jnp.transpose(result[: ROUNDS + 1], (0, 1, 3, 2, 4))
    return jnp.concatenate([below, result[ROUNDS + 1 :]], axis=0)


def solution(mesh):
    count = mesh.shape["sta"]
    return jax.shard_map(
        functools.partial(per_device, count),
        mesh=mesh,
        in_specs=(P(("days", "sta"), None, None), P(("days", "sta"), None), P(("days", "sta"), None)),
        out_specs=P(None, None, ("days", "sta"), None, None),
        check_vma=False,
    )
```

```python
import functools

import jax
import jax.numpy as jnp
import numpy as np
from jax import lax
from jax.experimental import pallas as pl
from jax.experimental.pallas import tpu as pltpu
from jax.sharding import PartitionSpec as P

ROUNDS = 3
TILE = 16
LANES = 128
PARTS = 3
COLS = 256
EARLY = 2
TURN = 4
EPSILON = 1e-06
NT = (((1,), (1,)), ((), ()))


def fourier_rows(samples):
    bins = samples // 2
    times = np.arange(samples, dtype=np.int32)
    phase = (times[:, None] * np.arange(bins, dtype=np.int32)[None, :]) % samples
    angle = np.float32(2.0 * np.pi / samples) * phase.astype(np.float32)
    half = times.astype(np.float32) + np.float32(0.5)
    taper = np.float32(0.5) - np.float32(0.5) * np.cos(np.float32(2.0 * np.pi / samples) * half)
    table = np.concatenate([taper[:, None] * np.cos(angle), -taper[:, None] * np.sin(angle)], axis=1)
    return jnp.asarray(np.ascontiguousarray(table.T), dtype=jnp.bfloat16)


def pick_rows(channels):
    out = np.zeros((2 * TILE, 2 * channels * TILE), np.float32)
    for part in range(2):
        for a in range(channels):
            start = (part * channels + a) * TILE
            out[part * TILE + a, start : start + TILE] = 1
    return jnp.asarray(out, dtype=jnp.bfloat16)


def spread_bins(channels, bins):
    row = np.arange(channels * TILE)
    col = np.arange(channels * bins)
    same = (row[:, None] // TILE == col[None, :] // bins) & (row[:, None] % TILE == col[None, :] % TILE)
    return jnp.asarray(same.astype(np.float32), dtype=jnp.bfloat16)


def kernel(
    dims, table_in, pick_in, spread_in, records_in, counts_in, gaps_in, result,
    table, pick, spread, records, counts, gaps,
    own, turned, inbox, weights, outgoing, returned,
    load_sem, send_sem, recv_sem, back_send, back_recv,
):
    channels, segments, samples, stations, hours, count = dims
    bins = samples // 2
    span = segments // hours
    groups = bins // TILE
    rows = channels * TILE
    per_station = channels // stations
    me = lax.axis_index("sta")
    kind = lax.rem(me, 4)
    core = lax.rem(kind, 2)
    far = kind // 3

    def at(offset):
        return lax.rem(me + offset + count, count)

    def barrier_signal():
        barrier = pltpu.get_barrier_semaphore()
        for offset in (1, 2, 3, 4, -1, -2, -3, -4):
            pl.semaphore_signal(
                barrier, inc=1, device_id={"sta": at(offset)}, device_id_type=pl.DeviceIdType.MESH
            )

    loads = [
        pltpu.make_async_copy(source, target, load_sem.at[i])
        for i, (source, target) in enumerate(
            (
                (table_in, table), (counts_in, counts), (gaps_in, gaps),
                (pick_in, pick), (spread_in, spread),
            )
        )
    ]
    for load in loads:
        load.start()
    record_loads = [
        pltpu.make_async_copy(records_in.at[c], records.at[c], load_sem.at[len(loads) + c])
        for c in range(channels)
    ]
    for load in record_loads:
        load.start()
    barrier_signal()
    part_rows = channels // PARTS
    for load in loads:
        load.wait()

    position = lax.broadcasted_iota(jnp.int32, (stations, segments), 1)
    limit = jnp.zeros((stations, segments), jnp.int32)
    for h in range(hours):
        limit = jnp.where(position // span == h, counts[:, h : h + 1], limit)
    valid = jnp.where(lax.rem(position, span) < limit, gaps[...], 0).astype(jnp.float32)
    valid = jnp.concatenate(
        [jnp.broadcast_to(valid[s : s + 1], (per_station, segments)) for s in range(stations)]
        + [jnp.zeros((TILE - channels, segments), jnp.float32)],
        axis=0,
    )
    left = lax.broadcasted_iota(jnp.int32, (TILE, LANES), 1) < span
    for pair in range(hours // 2):
        block = valid[:, pair * LANES : (pair + 1) * LANES]
        first = jnp.where(left, block, 0.0)
        second = jnp.where(left, pltpu.roll(block, span, 1), 0.0)
        own[0, :, 2 * pair * LANES : (2 * pair + 1) * LANES] = first.astype(jnp.bfloat16)
        own[0, :, (2 * pair + 1) * LANES : (2 * pair + 2) * LANES] = second.astype(jnp.bfloat16)

    def where_is(piece):
        if isinstance(piece, int) and piece == 0:
            return pl.ds(0, 1)
        return pl.ds(1 + (piece - 1) * part_rows, part_rows)

    def copy(source, piece, way, slot, target):
        return pltpu.make_async_remote_copy(
            src_ref=source.at[where_is(piece)],
            dst_ref=inbox.at[slot, where_is(piece)],
            send_sem=send_sem.at[way, piece],
            recv_sem=recv_sem.at[slot, piece],
            device_id={"sta": target},
            device_id_type=pl.DeviceIdType.MESH,
        )

    def ahead(piece):
        return copy(own, piece, 0, 1 + 2 * far, at(2 + 2 * far))

    def beside(piece):
        return copy(own, piece, 1, 2 * core, at(1 + 2 * core))

    def relay_twin(piece):
        return copy(inbox.at[1], piece, 2, 2 - 2 * core, at(1 - 2 * core))

    def relay_down(piece):
        return copy(inbox.at[3], piece, 3, 1, at(-2))

    def relay_twin_far(piece):
        return copy(inbox.at[3], piece, 1, 2, at(-1))

    def arrived(slot, piece):
        copy(own, piece, 0, slot, at(1)).wait_recv()

    def send_own(piece):
        ahead(piece).start()

        @pl.when(far == 0)
        def _():
            beside(piece).start()

    def pass_on(piece):
        @pl.when(far == 1)
        def _():
            arrived(3, piece)
            relay_down(piece).start()
            relay_twin_far(piece).start()

        arrived(1, piece)
        relay_twin(piece).start()

    left_b = lax.broadcasted_iota(jnp.int32, (bins, LANES), 1) < span

    def whiten(c):
        record_loads[c].wait()
        spectrum = lax.dot_general(table[...], records[c], NT, preferred_element_type=jnp.float32)
        power = jnp.sum(spectrum * spectrum, axis=0, keepdims=True) * (1.0 / samples)
        white = spectrum * (lax.rsqrt(power + EPSILON) * valid[c : c + 1])
        for pair in range(hours // 2):
            re = white[:bins, pair * LANES : (pair + 1) * LANES]
            im = white[bins:, pair * LANES : (pair + 1) * LANES]
            straight = (
                jnp.where(left_b, re, pltpu.roll(im, span, 1)),
                jnp.where(left_b, pltpu.roll(re, span, 1), im),
            )
            for half in range(2):
                lanes = slice((2 * pair + half) * LANES, (2 * pair + half + 1) * LANES)
                flat = straight[half].astype(jnp.bfloat16)
                for g in range(groups):
                    own[1 + g * channels + c, :, lanes] = flat[g * TILE : (g + 1) * TILE]

    early = min(EARLY, groups)
    for part in range(PARTS):
        for c in range(part * part_rows, (part + 1) * part_rows):
            whiten(c)
        if part == 0:
            pl.semaphore_wait(pltpu.get_barrier_semaphore(), 8)
            send_own(0)
        for g in range(early):
            send_own(1 + g * PARTS + part)
    for piece in range(early * PARTS, groups * PARTS):
        send_own(1 + piece)

    sign = jnp.where(left, 1.0, -1.0)

    @pl.loop(0, groups * channels // TURN)
    def _(i):
        for r in range(TURN):
            for h in range(hours):
                lanes = slice(h * LANES, (h + 1) * LANES)
                block = own[1 + i * TURN + r, :, lanes].astype(jnp.float32)
                turned[i * TURN + r, :, lanes] = (pltpu.roll(block, span, 1) * sign).astype(jnp.bfloat16)

    def dot_nt(a, b):
        return lax.dot_general(a, b, NT, preferred_element_type=jnp.float32)

    partners = (own,) + tuple(inbox.at[d] for d in range(ROUNDS))
    chunks = (ROUNDS + 1) * rows // COLS
    each = COLS // TILE

    def columns(blocks, n):
        out = []
        for d, block in enumerate(blocks):
            first = max(each * n, d * channels) - d * channels
            last = min(each * (n + 1), (d + 1) * channels) - d * channels
            if first < last:
                out.append(block[first * TILE : last * TILE])
        return jnp.concatenate(out, axis=0) if len(out) > 1 else out[0]

    def widen(ref, h):
        block = ref[0, :, h * LANES : (h + 1) * LANES].astype(jnp.float32)
        return jnp.concatenate(
            [jnp.broadcast_to(block[c : c + 1], (TILE, LANES)) for c in range(channels)], axis=0
        ).astype(jnp.bfloat16)

    def weigh():
        row_id = lax.broadcasted_iota(jnp.int32, (rows, COLS), 0)
        col_id = lax.broadcasted_iota(jnp.int32, (rows, COLS), 1)
        diagonal = lax.rem(row_id, TILE) == lax.rem(col_id, TILE)
        for h in range(hours):
            wide = [widen(ref, h) for ref in partners]
            for n in range(chunks):
                joint = dot_nt(wide[0], columns(wide, n))
                weights[h, n] = jnp.where(diagonal, 1.0 / (hours * jnp.maximum(joint, 1.0)), 0.0)

    def correlate(g):
        at_rows = pl.ds(1 + g * channels, channels)
        t_rows = pl.ds(g * channels, channels)
        picked = []
        for n in range(chunks):
            re = jnp.zeros((rows, COLS), jnp.float32)
            im = jnp.zeros((rows, COLS), jnp.float32)
            for h in range(hours):
                lanes = slice(h * LANES, (h + 1) * LANES)
                blocks = [ref[at_rows, :, lanes].reshape(rows, LANES) for ref in partners]
                mine_t = turned[t_rows, :, lanes].reshape(rows, LANES)
                product = dot_nt(jnp.concatenate([blocks[0], mine_t], axis=0), columns(blocks, n))
                scale = weights[h, n]
                re = re + product[:rows] * scale
                im = im + product[rows:] * scale
            both = jnp.concatenate([re, im], axis=0).astype(jnp.bfloat16)
            picked.append(jnp.dot(pick[...], both, preferred_element_type=jnp.float32))
        return jnp.concatenate(picked, axis=1)

    tall = 2 * TILE

    def give_back(d, g):
        return pltpu.make_async_remote_copy(
            src_ref=outgoing.at[g, pl.ds(d * tall, tall)],
            dst_ref=returned.at[g, pl.ds((d - 1) * tall, tall)],
            send_sem=back_send.at[d - 1, g],
            recv_sem=back_recv.at[d - 1, g],
            device_id={"sta": at(-d)},
            device_id_type=pl.DeviceIdType.MESH,
        )

    def finish(ref, slots):
        height = len(slots) * tall
        group_of = lax.rem(lax.broadcasted_iota(jnp.int32, (height, COLS), 1), bins) // TILE
        flat = ref[...].reshape(groups * height, rows)
        for n in range(channels * bins // COLS):
            wide = jnp.dot(
                flat, spread[:, n * COLS : (n + 1) * COLS], preferred_element_type=jnp.float32
            )
            merged = wide[:height]
            for g in range(1, groups):
                merged = jnp.where(group_of == g, wide[g * height : (g + 1) * height], merged)
            for i, (slot, flip) in enumerate(slots):
                for part in range(2):
                    for k in range(COLS // bins):
                        start = i * tall + part * TILE
                        value = merged[start : start + TILE, k * bins : (k + 1) * bins]
                        if flip and part == 1:
                            value = -value
                        result[slot, part, n * (COLS // bins) + k] = value.astype(jnp.bfloat16)

    pass_on(0)
    arrived(0, 0)
    arrived(2, 0)
    weigh()

    @pl.loop(0, groups)
    def _(g):
        pieces = [1 + g * PARTS + part for part in range(PARTS)]
        for piece in pieces:
            pass_on(piece)
        for piece in pieces:
            arrived(0, piece)
            arrived(2, piece)
        picked = correlate(g)
        for d in range(1, ROUNDS + 1):
            outgoing[g, d * tall : (d + 1) * tall] = picked[:, d * rows : (d + 1) * rows].astype(
                jnp.bfloat16
            )
            give_back(d, g).start()
        outgoing[g, :tall] = picked[:, :rows].astype(jnp.bfloat16)

    finish(outgoing, [(ROUNDS - d, False) for d in range(ROUNDS + 1)])

    @pl.loop(0, groups)
    def _(g):
        for d in range(1, ROUNDS + 1):
            give_back(d, g).wait_recv()

    finish(returned, [(ROUNDS + d, True) for d in range(1, ROUNDS + 1)])

    @pl.loop(0, groups)
    def _(g):
        for d in range(1, ROUNDS + 1):
            give_back(d, g).wait_send()

    def sent(piece):
        ahead(piece).wait_send()
        beside(piece).wait_send()
        relay_twin(piece).wait_send()

        @pl.when(far == 1)
        def _():
            relay_down(piece).wait_send()

    sent(0)

    @pl.loop(0, groups * PARTS)
    def _(i):
        sent(i + 1)


def per_device(count, records, counts, gap_mask):
    channels, segments, samples = records.shape
    stations, hours = counts.shape
    bins = samples // 2
    groups = bins // TILE
    rows = channels * TILE
    blocks = 1 + groups * channels
    wide = hours * LANES
    dims = (channels, segments, samples, stations, hours, count)
    pieces = groups * PARTS + 1
    result = pl.pallas_call(
        functools.partial(kernel, dims),
        out_shape=jax.ShapeDtypeStruct((2 * ROUNDS + 1, 2, channels, TILE, bins), jnp.bfloat16),
        in_specs=[pl.BlockSpec(memory_space=pltpu.HBM)] * 6,
        out_specs=pl.BlockSpec(memory_space=pltpu.VMEM),
        scratch_shapes=[
            pltpu.VMEM((samples, samples), jnp.bfloat16),
            pltpu.VMEM((2 * TILE, 2 * rows), jnp.bfloat16),
            pltpu.VMEM((rows, channels * bins), jnp.bfloat16),
            pltpu.VMEM((channels, segments, samples), jnp.bfloat16),
            pltpu.VMEM((stations, hours), jnp.int32),
            pltpu.VMEM((stations, segments), jnp.int32),
            pltpu.VMEM((blocks, TILE, wide), jnp.bfloat16),
            pltpu.VMEM((blocks - 1, TILE, wide), jnp.bfloat16),
            pltpu.VMEM((ROUNDS + 1, blocks, TILE, wide), jnp.bfloat16),
            pltpu.VMEM((hours, (ROUNDS + 1) * rows // COLS, rows, COLS), jnp.float32),
            pltpu.VMEM((groups, (ROUNDS + 1) * 2 * TILE, rows), jnp.bfloat16),
            pltpu.VMEM((groups, ROUNDS * 2 * TILE, rows), jnp.bfloat16),
            pltpu.SemaphoreType.DMA((5 + channels,)),
            pltpu.SemaphoreType.DMA((4, pieces)),
            pltpu.SemaphoreType.DMA((4, pieces)),
            pltpu.SemaphoreType.DMA((ROUNDS, groups)),
            pltpu.SemaphoreType.DMA((ROUNDS, groups)),
        ],
        compiler_params=pltpu.CompilerParams(
            collective_id=0, has_side_effects=True, vmem_limit_bytes=54 * 1024 * 1024
        ),
    )(
        fourier_rows(samples), pick_rows(channels), spread_bins(channels, bins),
        records, counts, gap_mask,
    )
    result = result[:, :, :, :channels]
    below = jnp.transpose(result[: ROUNDS + 1], (0, 1, 3, 2, 4))
    return jnp.concatenate([below, result[ROUNDS + 1 :]], axis=0)


def solution(mesh):
    count = mesh.shape["sta"]
    return jax.shard_map(
        functools.partial(per_device, count),
        mesh=mesh,
        in_specs=(P(("days", "sta"), None, None), P(("days", "sta"), None), P(("days", "sta"), None)),
        out_specs=P(None, None, ("days", "sta"), None, None),
        check_vma=False,
    )
```
